32 devices in a mesh: groups: 2 (over y), latent: 4 (over z), dp: 2 (over x), mp: 2 (over core).
Axes of the slice: x: 2, y: 2, z: 4, core: 2. Of those that a mesh axis runs over, the one named last changes fastest.
Arguments:
- tokens: bfloat16 [768, 8192], P(('groups', 'latent'), ('dp', 'mp')), parts along dimension 0, may hold values from -6 to 6
- active_latent_index: int32 [768, 64], P(('groups', 'latent')), parts along dimension 0, may hold values from 0 to 8191, as said below
- latent_values: bfloat16 [768, 64], P(('groups', 'latent')), parts along dimension 0, may hold values from 0.19921875 to 2
- dec_bias: float32 [16384], P(('groups', 'dp', 'mp')), parts along dimension 0, may hold values from -3 to 3
- dec_weight: bfloat16 [16384, 8192], P(('groups', 'latent'), ('dp', 'mp')), parts along dimension 0, may hold values from -0.75 to 0.75
Outputs:
- token_error: bfloat16 [768, 8192], P(('groups', 'latent'), ('dp', 'mp')), parts along dimension 0
- dec_grad: bfloat16 [16384, 8192], P(('groups', 'latent'), ('dp', 'mp')), parts along dimension 0
The draws below stay inside these ranges and needn't reach their ends.
There are 2 independent parts, one for each index of `groups`. The reference program is written for one: setup_inputs(seed, part) draws one part's arguments, and reference() takes and returns one part's arrays. A program takes and returns all parts, laid end to end along the dimension named above; each array names one. Nothing has to cross between parts.
Inputs may be any that keep to these rules, and one draw needn't show every extreme that they name: `active_latent_index`: each row names 64 different latents; where 384 * 64 >= 8192, every latent is named by some row.
All inputs are finite; a program needn't handle non-finite values.
Results may differ from the reference program's by a relative error of at most 0.0041.
Values may be sent and summed in bfloat16 or wider, within the bound.
No kernel may reach another device: no remote copies, remote signals or barrier semaphores. Data moves between devices by JAX's collectives and lax.ppermute only.
A program may use at most 64 MiB of HBM per device.

```python
import jax
import jax.numpy as jnp
from jax import lax

D = 8192
K = 64
TOK_SHARD = 96
LATENTS = 8192
TOKENS = 384
N_LATENT = 4


def draw_active_latent_index(key, part):
    key = jax.random.fold_in(key, 11)
    sorting_key, offset_key = jax.random.split(key)
    order = jax.random.permutation(sorting_key, LATENTS).astype(jnp.int32)
    row_index = jnp.arange(TOKENS, dtype=jnp.int32)
    drawn_offset = jax.random.randint(offset_key, (TOKENS,), 0, LATENTS, dtype=jnp.int32)
    covering = row_index * K < LATENTS
    start = jnp.where(covering, row_index * K, drawn_offset)
    slots = (start[:, None] + jnp.arange(K, dtype=jnp.int32)[None, :]) % LATENTS
    return order[slots]


def steps_of(stream_key, extent, cuts, low, top_value):
    level, own = 1.0, jax.random.fold_in(stream_key, 6)
    for position, parts in cuts:
        steps = jnp.exp(jax.random.uniform(jax.random.fold_in(own, position), (parts,), jnp.float32, low / len(cuts), top_value / len(cuts)))
        level = level * jnp.repeat(steps, extent[position] // parts).reshape([-1 if axis == position else 1 for axis in range(len(extent))])
    return level


def scatter_about(rng, dims, deviation, most, pieces=(), held_as=jnp.bfloat16):
    array = jax.random.normal(rng, dims, jnp.float32) * deviation
    if len(pieces) > 0:
        array = steps_of(rng, dims, pieces, -0.22, 0.18) * array
    return jnp.clip(array, min=-most, max=most).astype(held_as)


def setup_inputs(seed: int = 0, part: int = 0) -> dict:
    key_of = jax.random.split(jax.random.key(seed), 6)
    part_splits = jax.random.split(jax.random.fold_in(key_of[5], part), 6)
    tokens = scatter_about(part_splits[0], (TOKENS, D), 1.0, 6.0, ((0, 4), (1, 4)))
    active_latent_index = draw_active_latent_index(jax.random.fold_in(jax.random.fold_in(key_of[5], part), 71), part)
    latent_values = jnp.clip(0.19921875 + 1.8007812 * jax.random.uniform(part_splits[2], (TOKENS, K), jnp.float32) ** steps_of(part_splits[2], (TOKENS, K), ((0, 4),), -0.2, 0.2), 0.19921875, 2.0).astype(jnp.bfloat16)
    dec_bias = scatter_about(part_splits[3], (D,), 0.5, 3.0, ((0, 4),), jnp.float32)
    dec_weight = scatter_about(part_splits[4], (LATENTS, D), K ** -0.5, 0.75, ((0, 4), (1, 4)))
    return dict(tokens=tokens, active_latent_index=active_latent_index, latent_values=latent_values, dec_bias=dec_bias, dec_weight=dec_weight)


def reference(tokens, active_latent_index, latent_values, dec_bias, dec_weight):
    id_blocks = active_latent_index.reshape(N_LATENT, TOK_SHARD, K)
    value_blocks = latent_values.reshape(N_LATENT, TOK_SHARD, K)
    token_blocks = tokens.reshape(N_LATENT, TOK_SHARD, D)

    def one_block(inputs):
        block_latent_index, block_latent_value, block_tokens = inputs
        selected_rows = jnp.take(dec_weight, block_latent_index, axis=0).astype(jnp.float32)
        decoded_output = jnp.einsum("wj,wjo->wo", block_latent_value.astype(jnp.float32), selected_rows)
        return (decoded_output + dec_bias - block_tokens.astype(jnp.float32)).astype(jnp.bfloat16)

    error_matrix = lax.map(one_block, (id_blocks, value_blocks, token_blocks))

    def accumulate(running, inputs):
        block_latent_index, block_latent_value, block_errors = inputs
        updates = block_latent_value.astype(jnp.float32)[:, :, None] * block_errors.astype(jnp.float32)[:, None, :]
        return running.at[block_latent_index.reshape(-1)].add(updates.reshape(-1, D)), None

    grads, unused = lax.scan(accumulate, jnp.zeros((LATENTS, D), jnp.float32), (id_blocks, value_blocks, error_matrix))
    return error_matrix.reshape(TOKENS, D), grads.astype(jnp.bfloat16)
```

```python
import functools

import jax
import jax.numpy as jnp
from jax import lax
from jax.experimental import pallas as pl
from jax.experimental.pallas import tpu as pltpu
from jax.sharding import PartitionSpec as P

LANES = 128
GROUP = 8
CHAINS = 2
VMEM_LIMIT = 48 * 1024 * 1024


def params(grid_dims=1):
    return pltpu.CompilerParams(
        vmem_limit_bytes=VMEM_LIMIT, dimension_semantics=("arbitrary",) * grid_dims
    )


def ring_order(count):
    return [0] + list(range(1, count, 2)) + list(range(count - 2 + count % 2, 0, -2))


def ring_shift(count, step):
    order = ring_order(count)
    return [(order[i], order[(i + step) % count]) for i in range(count)]


def pack_kernel(ids_ref, values_ref, out_ref, wide_ref):
    rows, active = ids_ref.shape
    half = rows // 2
    wide_ref[0:rows, :] = ids_ref[...].astype(jnp.float32)
    wide_ref[rows:, :] = values_ref[...].astype(jnp.float32)
    even = wide_ref[pl.ds(0, 2 * half, stride=2), :]
    odd = wide_ref[pl.ds(1, 2 * half, stride=2), :]
    out_ref[...] = jnp.concatenate([even, odd], axis=1)


def pack(ids, values):
    rows, active = ids.shape
    return pl.pallas_call(
        pack_kernel,
        out_shape=jax.ShapeDtypeStruct((rows, 2 * active), jnp.float32),
        scratch_shapes=[pltpu.VMEM((2 * rows, active), jnp.float32)],
        compiler_params=params(0),
        name="pack",
    )(ids, values)


def build_table(first, packed_ref, table_ref, row0, keys_ref, width):
    rows = packed_ref.shape[0]
    half = rows // 2
    per_row = 2
    rows_per_group = GROUP // per_row
    high_count = width // LANES
    ids = packed_ref[0:half, :].astype(jnp.int32) - first
    high = lax.shift_right_arithmetic(ids, 7)
    low = jnp.bitwise_and(ids, LANES - 1)
    row = lax.broadcasted_iota(jnp.int32, ids.shape, 0)
    lane = lax.broadcasted_iota(jnp.int32, ids.shape, 1)
    place = per_row * jnp.bitwise_and(row, rows_per_group - 1) + jnp.where(lane >= LANES // 2, 1, 0)
    inside = jnp.logical_and(ids >= 0, ids < width)
    key = jnp.where(inside, high * GROUP + place, -1)
    keys_ref[0:half, :] = key.astype(jnp.float32)
    keys_ref[half : 2 * half, :] = low.astype(jnp.float32)
    tall = lax.broadcasted_iota(jnp.int32, (high_count * GROUP, LANES), 0).astype(jnp.float32).astype(jnp.bfloat16)
    wide = lax.broadcasted_iota(jnp.int32, (LANES, LANES), 0).astype(jnp.float32).astype(jnp.bfloat16)
    zero, one = jnp.zeros((), jnp.bfloat16), jnp.ones((), jnp.bfloat16)

    def group_rows(r0):
        left, right = [], []
        for j in range(rows_per_group):
            key = keys_ref[pl.ds(r0 + j, 1), :].astype(jnp.bfloat16)
            low = keys_ref[pl.ds(half + r0 + j, 1), :].astype(jnp.bfloat16)
            value = packed_ref[pl.ds(half + r0 + j, 1), :].astype(jnp.bfloat16)
            left.append(jnp.where(tall == key, value, zero))
            right.append(jnp.where(wide == low, one, zero))
        left = jnp.concatenate(left, axis=1)
        right = jnp.concatenate(right, axis=1)
        product = lax.dot_general(left, right, (((1,), (1,)), ((), ())), preferred_element_type=jnp.float32)
        pieces = [product[h * GROUP : (h + 1) * GROUP, :] for h in range(high_count)]
        return jnp.concatenate(pieces, axis=1)

    @pl.loop(0, rows // (2 * GROUP))
    def _(i):
        r0 = i * (2 * rows_per_group)
        both = jnp.concatenate([group_rows(r0), group_rows(r0 + rows_per_group)], axis=0)
        table_ref[pl.ds(pl.multiple_of(row0 + i * 2 * GROUP, 2 * GROUP), 2 * GROUP), :] = both.astype(jnp.bfloat16)


def partial_kernel(blocks, build, wire, first_ref, *refs):
    if build:
        packed, (weight_ref, table_ref), refs = refs[:blocks], refs[blocks : blocks + 2], refs[blocks + 2 :]
        outs, keys_ref = refs[:blocks], refs[blocks]
        rows = packed[0].shape[0]

        @pl.when(pl.program_id(0) == 0)
        def _():
            for b in range(blocks):
                build_table(first_ref[0], packed[b], table_ref, b * rows, keys_ref, weight_ref.shape[0])
    else:
        (table_ref, weight_ref), outs = refs[:2], refs[2:]
        rows = table_ref.shape[0] // blocks
    product = jnp.dot(table_ref[...], weight_ref[...], preferred_element_type=jnp.float32)
    for b in range(blocks):
        outs[b][...] = product[b * rows : (b + 1) * rows, :].astype(outs[b].dtype)


def partial_sums(first, packed, table, weight, chain, chains, wire, tile=256):
    build = table is None
    width, features = weight.shape
    columns = features // chains
    blocks = len(packed)
    rows = packed[0].shape[0]
    tile = min(tile, columns)
    base = chain * (columns // tile)
    whole = lambda shape: pl.BlockSpec(shape, lambda i, f: (0, 0))
    weight_spec = pl.BlockSpec((width, tile), lambda i, f: (0, base + i))
    table_shape = jax.ShapeDtypeStruct((blocks * rows, width), jnp.bfloat16)
    out_shapes = [
        jax.ShapeDtypeStruct((rows, columns), jnp.bfloat16 if b < wire else jnp.float32) for b in range(blocks)
    ]
    out_specs = [pl.BlockSpec((rows, tile), lambda i, f: (0, i)) for b in range(blocks)]
    if build:
        in_specs = [whole(p.shape) for p in packed] + [weight_spec]
        operands = (*packed, weight)
        out_shapes = [table_shape] + out_shapes
        out_specs = [whole(table_shape.shape)] + out_specs
        scratch = [pltpu.VMEM(packed[0].shape, jnp.float32)]
    else:
        in_specs = [whole(table_shape.shape), weight_spec]
        operands = (table, weight)
        scratch = []
    flops = 2 * blocks * rows * width * columns
    result = pl.pallas_call(
        functools.partial(partial_kernel, blocks, build, wire),
        grid_spec=pltpu.PrefetchScalarGridSpec(
            num_scalar_prefetch=1,
            grid=(columns // tile,),
            in_specs=in_specs,
            out_specs=out_specs,
            scratch_shapes=scratch,
        ),
        out_shape=out_shapes,
        compiler_params=params(),
        cost_estimate=pl.CostEstimate(flops=flops, bytes_accessed=2 * width * columns, transcendentals=0),
        name="partial_build" if build else "partial",
    )(first, *operands)
    if build:
        return result[0], list(result[1:])
    return table, list(result)


def grad_kernel(blocks, table_ref, *refs):
    errors, out_ref, all_ref = refs[:blocks], refs[-2], refs[-1]
    rows = errors[0].shape[0]

    @pl.when(pl.program_id(0) == 0)
    def _():
        for b in range(blocks):
            all_ref[b * rows : (b + 1) * rows, :] = errors[b][...]

    out_ref[...] = jnp.dot(table_ref[...], all_ref[...], preferred_element_type=jnp.float32).astype(out_ref.dtype)


def grad_part(table_t, errors, features, chain, previous, tile=512):
    width, tokens = table_t.shape
    rows, columns = errors[0].shape
    blocks = len(errors)
    in_specs = [pl.BlockSpec((tile, tokens), lambda i: (i, 0))] + [
        pl.BlockSpec((rows, columns), lambda i: (0, 0)) for _ in errors
    ]
    operands = [table_t, *errors]
    aliases = {}
    if previous is not None:
        in_specs.append(pl.BlockSpec(memory_space=pl.ANY))
        operands.append(previous)
        aliases = {len(operands) - 1: 0}
    return pl.pallas_call(
        functools.partial(grad_kernel, blocks),
        grid=(width // tile,),
        in_specs=in_specs,
        out_specs=pl.BlockSpec((tile, columns), lambda i: (i, chain)),
        out_shape=jax.ShapeDtypeStruct((width, features), jnp.bfloat16),
        scratch_shapes=[pltpu.VMEM((tokens, columns), jnp.bfloat16)],
        input_output_aliases=aliases,
        compiler_params=params(),
        cost_estimate=pl.CostEstimate(
            flops=2 * width * tokens * columns, bytes_accessed=2 * width * columns, transcendentals=0
        ),
        name="grad",
    )(*operands)


def local(count, tokens, active_latent_index, latent_values, dec_bias, dec_weight):
    width, features = dec_weight.shape
    columns = features // CHAINS
    first = (lax.axis_index("latent") * width).astype(jnp.int32).reshape(1)

    def send(x, step=1):
        return lax.ppermute(x, "latent", ring_shift(count, step))

    own = pack(active_latent_index, latent_values)
    others = [send(own, k) for k in range(1, count)]
    own_table, own_first = partial_sums(first, [own], None, dec_weight, 0, 1, 0)
    own_sum = own_first[0]
    other_table, sums = None, []
    for c in range(CHAINS):
        other_table, parts = partial_sums(first, others, other_table, dec_weight, c, CHAINS, 1)
        sums.append(parts)
    running = [sums[c][0] for c in range(CHAINS)]
    for step in range(1, count):
        for c in range(CHAINS):
            running[c] = send(running[c])
            if step < count - 1:
                running[c] = (running[c].astype(jnp.float32) + sums[c][step]).astype(jnp.bfloat16)
    errors = []
    for c in range(CHAINS):
        at = slice(c * columns, (c + 1) * columns)
        total = running[c].astype(jnp.float32) + own_sum[:, at] + dec_bias[at] - tokens[:, at].astype(jnp.float32)
        errors.append([total.astype(jnp.bfloat16)])
    for step in range(1, count):
        for c in range(CHAINS):
            errors[c].append(send(errors[c][-1]))
    table_t = jnp.concatenate([own_table, other_table], axis=0).T
    grad = None
    for c in range(CHAINS):
        grad = grad_part(table_t, errors[c], features, c, grad)
    token_error = jnp.concatenate([errors[c][0] for c in range(CHAINS)], axis=1)
    return token_error, grad


def solution(mesh):
    in_specs = (
        P(("groups", "latent"), ("dp", "mp")),
        P(("groups", "latent"), None),
        P(("groups", "latent"), None),
        P(("groups", "dp", "mp")),
        P(("groups", "latent"), ("dp", "mp")),
    )
    out_specs = (P(("groups", "latent"), ("dp", "mp")), P(("groups", "latent"), ("dp", "mp")))
    body = functools.partial(local, mesh.shape["latent"])
    return jax.shard_map(body, mesh=mesh, in_specs=in_specs, out_specs=out_specs, check_vma=False)
```

```python
import functools

import jax
import jax.numpy as jnp
from jax import lax
from jax.experimental import pallas as pl
from jax.experimental.pallas import tpu as pltpu
from jax.sharding import PartitionSpec as P

LANES = 128
GROUP = 8
CHAINS = 2
TILE = 512
VMEM_LIMIT = 24 * 1024 * 1024
IN_VMEM = pl.BlockSpec(memory_space=pltpu.VMEM)
IN_SMEM = pl.BlockSpec(memory_space=pltpu.SMEM)
IN_PLACE = pl.BlockSpec(memory_space=pl.ANY)


def params():
    return pltpu.CompilerParams(vmem_limit_bytes=VMEM_LIMIT)


def cost(byte_count):
    return pl.CostEstimate(flops=0, bytes_accessed=byte_count, transcendentals=0)


def ring_order(count):
    return [0] + list(range(1, count, 2)) + list(range(count - 2 + count % 2, 0, -2))


def ring_shift(count, step):
    order = ring_order(count)
    return [(order[i], order[(i + step) % count]) for i in range(count)]


def pack_kernel(ids_ref, values_ref, out_ref, wide_ref):
    active, rows = ids_ref.shape
    wide_ref[0:rows, :] = ids_ref[...].astype(jnp.float32).T
    wide_ref[rows:, :] = values_ref[...].astype(jnp.float32).T
    even = wide_ref[pl.ds(0, rows, stride=2), :]
    odd = wide_ref[pl.ds(1, rows, stride=2), :]
    out_ref[...] = jnp.concatenate([even, odd], axis=1)


def pack(ids, values):
    rows, active = ids.shape
    return pl.pallas_call(
        pack_kernel,
        in_specs=[IN_VMEM, IN_VMEM],
        out_specs=IN_VMEM,
        out_shape=jax.ShapeDtypeStruct((rows, 2 * active), jnp.float32),
        scratch_shapes=[pltpu.VMEM((2 * rows, active), jnp.float32)],
        compiler_params=params(),
        cost_estimate=cost(32 * 1024 * 1024),
        name="pack",
    )(ids.T, values.T)


def build_table(first, packed_ref, table_ref, keys_ref):
    rows, width = table_ref.shape
    half = rows // 2
    per_row = 2
    rows_per_group = GROUP // per_row
    high_count = width // LANES
    ids = packed_ref[0:half, :].astype(jnp.int32) - first
    high = lax.shift_right_arithmetic(ids, 7)
    low = jnp.bitwise_and(ids, LANES - 1)
    row = lax.broadcasted_iota(jnp.int32, ids.shape, 0)
    lane = lax.broadcasted_iota(jnp.int32, ids.shape, 1)
    place = per_row * jnp.bitwise_and(row, rows_per_group - 1) + jnp.where(lane >= LANES // 2, 1, 0)
    inside = jnp.logical_and(ids >= 0, ids < width)
    key = jnp.where(inside, high * GROUP + place, -1)
    keys_ref[0:half, :] = key.astype(jnp.float32)
    keys_ref[half : 2 * half, :] = low.astype(jnp.float32)
    tall = lax.broadcasted_iota(jnp.int32, (high_count * GROUP, LANES), 0).astype(jnp.float32).astype(jnp.bfloat16)
    wide = lax.broadcasted_iota(jnp.int32, (LANES, LANES), 0).astype(jnp.float32).astype(jnp.bfloat16)
    zero, one = jnp.zeros((), jnp.bfloat16), jnp.ones((), jnp.bfloat16)

    def group_rows(r0):
        left, right = [], []
        for r in range(r0, r0 + rows_per_group):
            key = keys_ref[r : r + 1, :].astype(jnp.bfloat16)
            low = keys_ref[half + r : half + r + 1, :].astype(jnp.bfloat16)
            value = packed_ref[half + r : half + r + 1, :].astype(jnp.bfloat16)
            left.append(jnp.where(tall == key, value, zero))
            right.append(jnp.where(wide == low, one, zero))
        left = jnp.concatenate(left, axis=1)
        right = jnp.concatenate(right, axis=1)
        product = lax.dot_general(left, right, (((1,), (1,)), ((), ())), preferred_element_type=jnp.float32)
        pieces = [product[h * GROUP : (h + 1) * GROUP, :] for h in range(high_count)]
        return jnp.concatenate(pieces, axis=1)

    for i in range(rows // (2 * GROUP)):
        r0 = i * (2 * rows_per_group)
        both = jnp.concatenate([group_rows(r0), group_rows(r0 + rows_per_group)], axis=0)
        table_ref[i * 2 * GROUP : (i + 1) * 2 * GROUP, :] = both.astype(jnp.bfloat16)


def multiply(table_ref, weight_ref, column0, columns, write):
    tile = min(TILE, columns)
    for c in range(0, columns, tile):
        product = jnp.dot(
            table_ref[...], weight_ref[:, column0 + c : column0 + c + tile], preferred_element_type=jnp.float32
        )
        write(slice(c, c + tile), product)


def build_kernel(blocks, column0, first_ref, *refs):
    packed, refs = refs[:blocks], refs[blocks:]
    if column0 is not None:
        weight_ref, refs = refs[0], refs[1:]
    tables, refs = refs[:blocks], refs[blocks:]
    for packed_ref, table_ref in zip(packed, tables):
        build_table(first_ref[0], packed_ref, table_ref, refs[-1])
    if column0 is not None:
        out_ref = refs[0]

        def write(at, product):
            out_ref[:, at] = product.astype(out_ref.dtype)

        multiply(tables[0], weight_ref, column0, out_ref.shape[1], write)


def build(first, packed, width, weight=None, column0=None, columns=None):
    blocks = len(packed)
    rows = packed[0].shape[0]
    tables = [jax.ShapeDtypeStruct((rows, width), jnp.bfloat16)] * blocks
    extra = [] if weight is None else [weight]
    sums = [] if weight is None else [jax.ShapeDtypeStruct((rows, columns), jnp.bfloat16)]
    return pl.pallas_call(
        functools.partial(build_kernel, blocks, column0),
        in_specs=[IN_SMEM] + [IN_VMEM] * (blocks + len(extra)),
        out_specs=[IN_VMEM] * (blocks + len(sums)),
        out_shape=tables + sums,
        scratch_shapes=[pltpu.VMEM(packed[0].shape, jnp.float32)],
        compiler_params=params(),
        cost_estimate=cost(1 << 20),
        name="build",
    )(first, *packed, *extra)


def partial_kernel(column0, added, table_ref, weight_ref, *refs):
    out_ref = refs[-1]

    def write(at, product):
        if added:
            product = product + refs[0][:, at].astype(jnp.float32)
        out_ref[:, at] = product.astype(out_ref.dtype)

    multiply(table_ref, weight_ref, column0, out_ref.shape[1], write)


def partial_sum(table, weight, column0, columns, arrived=None):
    extra = [] if arrived is None else [arrived]
    return pl.pallas_call(
        functools.partial(partial_kernel, column0, len(extra)),
        in_specs=[IN_VMEM] * (2 + len(extra)),
        out_specs=IN_VMEM,
        out_shape=jax.ShapeDtypeStruct((table.shape[0], columns), jnp.bfloat16),
        compiler_params=params(),
        cost_estimate=cost(1 << 20),
        name="partial_sum",
    )(table, weight, *extra)


def error_kernel(column0, table_ref, weight_ref, arrived_ref, bias_ref, tokens_ref, out_ref):
    def write(at, product):
        where = slice(column0 + at.start, column0 + at.stop)
        total = product + arrived_ref[:, at].astype(jnp.float32) + bias_ref[:, where]
        out_ref[:, at] = (total - tokens_ref[:, where].astype(jnp.float32)).astype(out_ref.dtype)

    multiply(table_ref, weight_ref, column0, out_ref.shape[1], write)


def token_errors(table, weight, column0, arrived, bias, tokens):
    return pl.pallas_call(
        functools.partial(error_kernel, column0),
        in_specs=[IN_VMEM] * 5,
        out_specs=IN_VMEM,
        out_shape=jax.ShapeDtypeStruct(arrived.shape, jnp.bfloat16),
        compiler_params=params(),
        cost_estimate=cost(1 << 20),
        name="token_errors",
    )(table, weight, arrived, bias, tokens)


def grad_kernel(blocks, column0, tile, table_ref, *refs):
    errors = refs[:blocks]
    out_ref, all_ref, made_ref, sems = refs[-4:]
    rows, columns = errors[0].shape
    for b in range(blocks):
        all_ref[b * rows : (b + 1) * rows, :] = errors[b][...]
    copies = []
    for i, c in enumerate(range(0, columns, tile)):
        product = jnp.dot(table_ref[...], all_ref[:, c : c + tile], preferred_element_type=jnp.float32)
        made_ref[:, c : c + tile] = product.astype(made_ref.dtype)
        copy = pltpu.make_async_copy(
            made_ref.at[:, pl.ds(c, tile)], out_ref.at[:, pl.ds(column0 + c, tile)], sems.at[i]
        )
        copy.start()
        copies.append(copy)
    for copy in copies:
        copy.wait()


def grad_part(table_t, errors, features, column0, previous, tile=256):
    width, tokens = table_t.shape
    rows, columns = errors[0].shape
    blocks = len(errors)
    tile = min(tile, columns)
    in_specs = [IN_VMEM] * (1 + blocks)
    operands = [table_t, *errors]
    aliases = {}
    if previous is not None:
        in_specs.append(IN_PLACE)
        operands.append(previous)
        aliases = {len(operands) - 1: 0}
    return pl.pallas_call(
        functools.partial(grad_kernel, blocks, column0, tile),
        in_specs=in_specs,
        out_specs=IN_PLACE,
        out_shape=jax.ShapeDtypeStruct((width, features), jnp.bfloat16),
        scratch_shapes=[
            pltpu.VMEM((tokens, columns), jnp.bfloat16),
            pltpu.VMEM((width, columns), jnp.bfloat16),
            pltpu.SemaphoreType.DMA((columns // tile,)),
        ],
        input_output_aliases=aliases,
        compiler_params=params(),
        cost_estimate=cost(1 << 20),
        name="grad",
    )(*operands)


def local(count, tokens, active_latent_index, latent_values, dec_bias, dec_weight):
    width, features = dec_weight.shape
    columns = features // CHAINS
    starts = [c * columns for c in range(CHAINS)]
    first = (lax.axis_index("latent") * width).astype(jnp.int32).reshape(1)
    bias = dec_bias.reshape(1, features)

    def send(x, step=1):
        return lax.ppermute(x, "latent", ring_shift(count, step))

    own = pack(active_latent_index, latent_values)
    packed = lax.optimization_barrier([own] + [send(own, k) for k in range(1, count)])
    tables = [None] * count
    tables[1], sent = build(first, [packed[1]], width, dec_weight, 0, columns)
    running = [sent] + [partial_sum(tables[1], dec_weight, at, columns) for at in starts[1:]]
    later = list(range(2, count)) + [0]
    last_sent, *waiting = lax.optimization_barrier([running[-1]] + [packed[k] for k in later])
    running[-1] = last_sent
    for k, table in zip(later, build(first, waiting, width)):
        tables[k] = table
    errors = [None] * CHAINS
    for k in later:
        for c, at in enumerate(starts):
            arrived = send(running[c])
            if k:
                running[c] = partial_sum(tables[k], dec_weight, at, columns, arrived)
            else:
                errors[c] = [token_errors(tables[k], dec_weight, at, arrived, bias, tokens)]
    for step in range(1, count):
        for c in range(CHAINS):
            errors[c].append(send(errors[c][-1]))
    table_t = jnp.concatenate(tables, axis=0).T
    grad = None
    for c, at in enumerate(starts):
        grad = grad_part(table_t, errors[c], features, at, grad)
    token_error = jnp.concatenate([errors[c][0] for c in range(CHAINS)], axis=1)
    return token_error, grad


def solution(mesh):
    in_specs = (
        P(("groups", "latent"), ("dp", "mp")),
        P(("groups", "latent"), None),
        P(("groups", "latent"), None),
        P(("groups", "dp", "mp")),
        P(("groups", "latent"), ("dp", "mp")),
    )
    out_specs = (P(("groups", "latent"), ("dp", "mp")), P(("groups", "latent"), ("dp", "mp")))
    body = functools.partial(local, mesh.shape["latent"])
    return jax.shard_map(body, mesh=mesh, in_specs=in_specs, out_specs=out_specs, check_vma=False)
```

```python
import functools

import jax
import jax.numpy as jnp
from jax import lax
from jax.experimental import pallas as pl
from jax.experimental.pallas import tpu as pltpu
from jax.sharding import PartitionSpec as P

LANES = 128
GROUP = 8
CHAINS = 2
TILE = 512
LOAD_PARTS = 8
VMEM_LIMIT = 24 * 1024 * 1024
IN_VMEM = pl.BlockSpec(memory_space=pltpu.VMEM)
IN_SMEM = pl.BlockSpec(memory_space=pltpu.SMEM)
IN_HBM = pl.BlockSpec(memory_space=pltpu.HBM)


def params():
    return pltpu.CompilerParams(vmem_limit_bytes=VMEM_LIMIT)


def in_hbm(array):
    return pltpu.with_memory_space_constraint(array, pltpu.HBM)


def cost(byte_count):
    return pl.CostEstimate(flops=0, bytes_accessed=byte_count, transcendentals=0)


def ring_order(count):
    return [0] + list(range(1, count, 2)) + list(range(count - 2 + count % 2, 0, -2))


def ring_shift(count, step):
    order = ring_order(count)
    return [(order[i], order[(i + step) % count]) for i in range(count)]


def pack_kernel(ids_in, values_in, out_ref, ids_ref, values_ref, wide_ref, sems):
    copies = [
        pltpu.make_async_copy(ids_in, ids_ref, sems.at[0]),
        pltpu.make_async_copy(values_in, values_ref, sems.at[1]),
    ]
    for copy in copies:
        copy.start()
    for copy in copies:
        copy.wait()
    active, rows = ids_ref.shape
    wide_ref[0:rows, :] = ids_ref[...].astype(jnp.float32).T
    wide_ref[rows:, :] = values_ref[...].astype(jnp.float32).T
    even = wide_ref[pl.ds(0, rows, stride=2), :]
    odd = wide_ref[pl.ds(1, rows, stride=2), :]
    out_ref[...] = jnp.concatenate([even, odd], axis=1)


def pack(ids, values):
    rows, active = ids.shape
    return pl.pallas_call(
        pack_kernel,
        in_specs=[IN_HBM, IN_HBM],
        out_specs=IN_VMEM,
        out_shape=jax.ShapeDtypeStruct((rows, 2 * active), jnp.float32),
        scratch_shapes=[
            pltpu.VMEM((active, rows), ids.dtype),
            pltpu.VMEM((active, rows), values.dtype),
            pltpu.VMEM((2 * rows, active), jnp.float32),
            pltpu.SemaphoreType.DMA((2,)),
        ],
        compiler_params=params(),
        cost_estimate=cost(1 << 20),
        name="pack",
    )(in_hbm(ids.T), in_hbm(values.T))


def build_table(first, packed_ref, table_ref, keys_ref):
    rows, width = table_ref.shape
    half = rows // 2
    per_row = 2
    rows_per_group = GROUP // per_row
    high_count = width // LANES
    ids = packed_ref[0:half, :].astype(jnp.int32) - first
    high = lax.shift_right_arithmetic(ids, 7)
    low = jnp.bitwise_and(ids, LANES - 1)
    row = lax.broadcasted_iota(jnp.int32, ids.shape, 0)
    lane = lax.broadcasted_iota(jnp.int32, ids.shape, 1)
    place = per_row * jnp.bitwise_and(row, rows_per_group - 1) + jnp.where(lane >= LANES // 2, 1, 0)
    inside = jnp.logical_and(ids >= 0, ids < width)
    key = jnp.where(inside, high * GROUP + place, -1)
    keys_ref[0:half, :] = key.astype(jnp.float32)
    keys_ref[half : 2 * half, :] = low.astype(jnp.float32)
    tall = lax.broadcasted_iota(jnp.int32, (high_count * GROUP, LANES), 0).astype(jnp.float32).astype(jnp.bfloat16)
    wide = lax.broadcasted_iota(jnp.int32, (LANES, LANES), 0).astype(jnp.float32).astype(jnp.bfloat16)
    zero, one = jnp.zeros((), jnp.bfloat16), jnp.ones((), jnp.bfloat16)

    def group_rows(r0):
        left, right = [], []
        for r in range(r0, r0 + rows_per_group):
            key = keys_ref[r : r + 1, :].astype(jnp.bfloat16)
            low = keys_ref[half + r : half + r + 1, :].astype(jnp.bfloat16)
            value = packed_ref[half + r : half + r + 1, :].astype(jnp.bfloat16)
            left.append(jnp.where(tall == key, value, zero))
            right.append(jnp.where(wide == low, one, zero))
        left = jnp.concatenate(left, axis=1)
        right = jnp.concatenate(right, axis=1)
        product = lax.dot_general(left, right, (((1,), (1,)), ((), ())), preferred_element_type=jnp.float32)
        pieces = [product[h * GROUP : (h + 1) * GROUP, :] for h in range(high_count)]
        return jnp.concatenate(pieces, axis=1)

    for i in range(rows // (2 * GROUP)):
        r0 = i * (2 * rows_per_group)
        both = jnp.concatenate([group_rows(r0), group_rows(r0 + rows_per_group)], axis=0)
        table_ref[i * 2 * GROUP : (i + 1) * 2 * GROUP, :] = both.astype(jnp.bfloat16)


def multiply(table_ref, weight_ref, write):
    columns = weight_ref.shape[1]
    tile = min(TILE, columns)
    for c in range(0, columns, tile):
        at = slice(c, c + tile)
        write(at, jnp.dot(table_ref[...], weight_ref[:, at], preferred_element_type=jnp.float32))


def load_and_multiply(weight_hbm, column0, weight_ref, sems, meanwhile, tables):
    width, columns = weight_ref.shape
    part = width // LOAD_PARTS
    spans = [slice(l, l + part) for l in range(0, width, part)]
    copies = [
        pltpu.make_async_copy(
            weight_hbm.at[pl.ds(at.start, part), pl.ds(column0, columns)],
            weight_ref.at[pl.ds(at.start, part), :],
            sems.at[i],
        )
        for i, at in enumerate(spans)
    ]
    for copy in copies:
        copy.start()
    meanwhile()
    total = None
    for copy, at in zip(copies, spans):
        copy.wait()
        stacked = jnp.concatenate([table_ref[:, at] for table_ref in tables], axis=0)
        product = jnp.dot(stacked, weight_ref[at, :], preferred_element_type=jnp.float32)
        total = product if total is None else total + product
    return total


def first_load_kernel(first_ref, packed_ref, weight_hbm, weight_ref, table_ref, out_ref, keys_ref, sems):
    def meanwhile():
        build_table(first_ref[0], packed_ref, table_ref, keys_ref)

    total = load_and_multiply(weight_hbm, 0, weight_ref, sems, meanwhile, [table_ref])
    out_ref[...] = total.astype(out_ref.dtype)


def first_load(first, packed, weight, columns):
    width = weight.shape[0]
    rows = packed.shape[0]
    return pl.pallas_call(
        first_load_kernel,
        in_specs=[IN_SMEM, IN_VMEM, IN_HBM],
        out_specs=[IN_VMEM] * 3,
        out_shape=[
            jax.ShapeDtypeStruct((width, columns), weight.dtype),
            jax.ShapeDtypeStruct((rows, width), jnp.bfloat16),
            jax.ShapeDtypeStruct((rows, columns), jnp.bfloat16),
        ],
        scratch_shapes=[pltpu.VMEM(packed.shape, jnp.float32), pltpu.SemaphoreType.DMA((LOAD_PARTS,))],
        compiler_params=params(),
        cost_estimate=cost(1 << 20),
        name="first_load",
    )(first, packed, in_hbm(weight))


def second_load_kernel(blocks, column0, first_ref, *refs):
    packed, (table1_ref, earlier_ref, weight_hbm) = refs[:blocks], refs[blocks : blocks + 3]
    outs = refs[blocks + 3 : -2]
    weight_ref, own_a_ref, own_b_ref, out_ref = outs[:4]
    tables = outs[4:]
    keys_ref, sems = refs[-2:]

    def meanwhile():
        for packed_ref, table_ref in zip(packed, tables):
            build_table(first_ref[0], packed_ref, table_ref, keys_ref)

        def write(at, product):
            own_a_ref[:, at] = product

        multiply(tables[0], earlier_ref, write)

    total = load_and_multiply(weight_hbm, column0, weight_ref, sems, meanwhile, [tables[0], table1_ref])
    rows = table1_ref.shape[0]
    own_b_ref[...] = total[:rows, :]
    out_ref[...] = total[rows:, :].astype(out_ref.dtype)


def second_load(first, packed, table1, earlier, weight):
    width, columns = earlier.shape
    rows = table1.shape[0]
    blocks = len(packed)
    wide = jax.ShapeDtypeStruct((rows, columns), jnp.float32)
    shapes = [jax.ShapeDtypeStruct((width, columns), weight.dtype), wide, wide]
    shapes += [jax.ShapeDtypeStruct((rows, columns), jnp.bfloat16)] + [table1] * blocks
    return pl.pallas_call(
        functools.partial(second_load_kernel, blocks, columns),
        in_specs=[IN_SMEM] + [IN_VMEM] * (blocks + 2) + [IN_HBM],
        out_specs=[IN_VMEM] * len(shapes),
        out_shape=[jax.ShapeDtypeStruct(x.shape, x.dtype) for x in shapes],
        scratch_shapes=[pltpu.VMEM(packed[0].shape, jnp.float32), pltpu.SemaphoreType.DMA((LOAD_PARTS,))],
        compiler_params=params(),
        cost_estimate=cost(1 << 20),
        name="second_load",
    )(first, *packed, table1, earlier, in_hbm(weight))


def partial_kernel(table_ref, weight_ref, arrived_ref, out_ref):
    def write(at, product):
        out_ref[:, at] = (product + arrived_ref[:, at].astype(jnp.float32)).astype(out_ref.dtype)

    multiply(table_ref, weight_ref, write)


def partial_sum(table, weight, arrived):
    return pl.pallas_call(
        partial_kernel,
        in_specs=[IN_VMEM] * 3,
        out_specs=IN_VMEM,
        out_shape=jax.ShapeDtypeStruct(arrived.shape, jnp.bfloat16),
        compiler_params=params(),
        cost_estimate=cost(1 << 20),
        name="partial_sum",
    )(table, weight, arrived)


def error_kernel(column0, arrived_ref, own_ref, bias_ref, tokens_ref, out_ref):
    part = slice(column0, column0 + out_ref.shape[1])
    total = arrived_ref[...].astype(jnp.float32) + own_ref[...] + bias_ref[:, part]
    out_ref[...] = (total - tokens_ref[:, part].astype(jnp.float32)).astype(out_ref.dtype)


def token_errors(column0, arrived, own_sum, bias, tokens):
    return pl.pallas_call(
        functools.partial(error_kernel, column0),
        in_specs=[IN_VMEM] * 4,
        out_specs=IN_VMEM,
        out_shape=jax.ShapeDtypeStruct(arrived.shape, jnp.bfloat16),
        compiler_params=params(),
        cost_estimate=cost(1 << 20),
        name="token_errors",
    )(arrived, own_sum, bias, tokens)


def grad_kernel(blocks, column0, tile, *refs):
    tables, errors = refs[:blocks], refs[blocks : 2 * blocks]
    error_out, grad_out, all_ref, made_ref, sems = refs[-5:]
    rows, columns = errors[0].shape
    width = tables[0].shape[1]
    at = pl.ds(column0, columns)
    copies = [pltpu.make_async_copy(errors[0], error_out.at[:, at], sems.at[width // tile])]
    copies[0].start()
    for b in range(blocks):
        all_ref[b * rows : (b + 1) * rows, :] = errors[b][...]
    for i, l in enumerate(range(0, width, tile)):
        table = jnp.concatenate([table_ref[:, l : l + tile] for table_ref in tables], axis=0)
        product = lax.dot_general(table, all_ref[...], (((0,), (0,)), ((), ())), preferred_element_type=jnp.float32)
        made_ref[l : l + tile, :] = product.astype(made_ref.dtype)
        copy = pltpu.make_async_copy(made_ref.at[pl.ds(l, tile), :], grad_out.at[pl.ds(l, tile), at], sems.at[i])
        copy.start()
        copies.append(copy)
    for copy in copies:
        copy.wait()


def grad_part(tables, errors, features, column0, previous, tile=256):
    width = tables[0].shape[1]
    rows, columns = errors[0].shape
    blocks = len(errors)
    in_specs = [IN_VMEM] * (2 * blocks)
    operands = [*tables, *errors]
    aliases = {}
    if previous is not None:
        aliases = {len(operands): 0, len(operands) + 1: 1}
        in_specs += [IN_HBM, IN_HBM]
        operands += previous
    return pl.pallas_call(
        functools.partial(grad_kernel, blocks, column0, tile),
        in_specs=in_specs,
        out_specs=[IN_HBM, IN_HBM],
        out_shape=[
            jax.ShapeDtypeStruct((rows, features), jnp.bfloat16),
            jax.ShapeDtypeStruct((width, features), jnp.bfloat16),
        ],
        scratch_shapes=[
            pltpu.VMEM((blocks * rows, columns), jnp.bfloat16),
            pltpu.VMEM((width, columns), jnp.bfloat16),
            pltpu.SemaphoreType.DMA((width // tile + 1,)),
        ],
        input_output_aliases=aliases,
        compiler_params=params(),
        cost_estimate=cost(1 << 20),
        name="grad",
    )(*operands)


def local(count, tokens, active_latent_index, latent_values, dec_bias, dec_weight):
    width, features = dec_weight.shape
    columns = features // CHAINS
    starts = [c * columns for c in range(CHAINS)]
    first = (lax.axis_index("latent") * width).astype(jnp.int32).reshape(1)
    def send(x, step=1):
        return lax.ppermute(x, "latent", ring_shift(count, step))

    own = pack(active_latent_index, latent_values)
    packed = [own] + [send(own, k) for k in range(1, count)]
    weight_a, table1, sent_a = first_load(first, packed[1], dec_weight, columns)
    made = second_load(first, packed[:1] + packed[2:], table1, weight_a, dec_weight)
    weights, own_sums, running = [weight_a, made[0]], made[1:3], [sent_a, made[3]]
    tables = [made[4], table1, *made[5:]]
    for k in range(2, count):
        for c in range(CHAINS):
            running[c] = partial_sum(tables[k], weights[c], send(running[c]))
    bias = dec_bias.reshape(1, features)
    errors = [[token_errors(at, send(running[c]), own_sums[c], bias, tokens)] for c, at in enumerate(starts)]
    for step in range(1, count):
        for c in range(CHAINS):
            errors[c].append(send(errors[c][-1]))
    made = None
    for c, at in enumerate(starts):
        made = grad_part(tables, errors[c], features, at, made)
    return tuple(made)


def solution(mesh):
    in_specs = (
        P(("groups", "latent"), ("dp", "mp")),
        P(("groups", "latent"), None),
        P(("groups", "latent"), None),
        P(("groups", "dp", "mp")),
        P(("groups", "latent"), ("dp", "mp")),
    )
    out_specs = (P(("groups", "latent"), ("dp", "mp")), P(("groups", "latent"), ("dp", "mp")))
    body = functools.partial(local, mesh.shape["latent"])
    return jax.shard_map(body, mesh=mesh, in_specs=in_specs, out_specs=out_specs, check_vma=False)
```

```python
import functools

import jax
import jax.numpy as jnp
from jax import lax
from jax.experimental import pallas as pl
from jax.experimental.pallas import tpu as pltpu
from jax.sharding import PartitionSpec as P

LANES = 128
EXPONENT_BITS = (1, 2, 4, 8, 16, 32, 64)
GROUP = 8
TILE = 512
LOAD_PARTS = 8
VMEM_LIMIT = 24 * 1024 * 1024
IN_VMEM = pl.BlockSpec(memory_space=pltpu.VMEM)
IN_SMEM = pl.BlockSpec(memory_space=pltpu.SMEM)
IN_HBM = pl.BlockSpec(memory_space=pltpu.HBM)


def params():
    return pltpu.CompilerParams(vmem_limit_bytes=VMEM_LIMIT)


def in_hbm(array):
    return pltpu.with_memory_space_constraint(array, pltpu.HBM)


def cost(byte_count):
    return pl.CostEstimate(flops=0, bytes_accessed=byte_count, transcendentals=0)


def ring_order(count):
    return [0] + list(range(1, count, 2)) + list(range(count - 2 + count % 2, 0, -2))


def ring_next(count):
    order = ring_order(count)
    return [(order[i], order[(i + 1) % count]) for i in range(count)]


def pack(ids, values, wide_ref):
    active, rows = ids.shape
    high = lax.shift_right_logical(ids, 7)
    low = jnp.bitwise_and(ids, LANES - 1)
    coded = 1.0 + low.astype(jnp.float32) * (1.0 / LANES)
    for bit in EXPONENT_BITS:
        coded = jnp.where(jnp.bitwise_and(high, bit) != 0, coded * 2.0**bit, coded)
    coded = jnp.where(high >= LANES, -coded, coded)
    wide_ref[0:rows, :] = coded.T
    wide_ref[rows:, :] = values.astype(jnp.float32).T
    even = wide_ref[pl.ds(0, rows, stride=2), :]
    odd = wide_ref[pl.ds(1, rows, stride=2), :]
    return jnp.concatenate([even, odd], axis=1)


def unpack_ids(coded):
    rest = jnp.abs(coded)
    high = jnp.where(coded < 0, LANES, 0)
    for bit in reversed(EXPONENT_BITS):
        over = rest >= 2.0**bit
        rest = jnp.where(over, rest * 2.0**-bit, rest)
        high = high + jnp.where(over, bit, 0)
    return high, ((rest - 1.0) * LANES).astype(jnp.int32)


def build_table(first, packed, table_ref, keys_ref):
    rows, width = table_ref.shape
    half = rows // 2
    per_row = 2
    rows_per_group = GROUP // per_row
    high_count = width // LANES
    high, low = unpack_ids(packed[0:half, :])
    high = high - first
    row = lax.broadcasted_iota(jnp.int32, high.shape, 0)
    lane = lax.broadcasted_iota(jnp.int32, high.shape, 1)
    place = per_row * jnp.bitwise_and(row, rows_per_group - 1) + jnp.where(lane >= LANES // 2, 1, 0)
    inside = jnp.logical_and(high >= 0, high < high_count)
    key = jnp.where(inside, high * GROUP + place, -1)
    keys_ref[0:half, :] = key.astype(jnp.float32)
    keys_ref[half : 2 * half, :] = low.astype(jnp.float32)
    keys_ref[2 * half :, :] = packed[half:, :]
    tall = lax.broadcasted_iota(jnp.int32, (high_count * GROUP, LANES), 0).astype(jnp.float32).astype(jnp.bfloat16)
    wide = lax.broadcasted_iota(jnp.int32, (LANES, LANES), 0).astype(jnp.float32).astype(jnp.bfloat16)
    zero, one = jnp.zeros((), jnp.bfloat16), jnp.ones((), jnp.bfloat16)

    def group_rows(r0):
        left, right = [], []
        for r in range(r0, r0 + rows_per_group):
            key = keys_ref[r : r + 1, :].astype(jnp.bfloat16)
            low = keys_ref[half + r : half + r + 1, :].astype(jnp.bfloat16)
            value = keys_ref[2 * half + r : 2 * half + r + 1, :].astype(jnp.bfloat16)
            left.append(jnp.where(tall == key, value, zero))
            right.append(jnp.where(wide == low, one, zero))
        left = jnp.concatenate(left, axis=1)
        right = jnp.concatenate(right, axis=1)
        product = lax.dot_general(left, right, (((1,), (1,)), ((), ())), preferred_element_type=jnp.float32)
        pieces = [product[h * GROUP : (h + 1) * GROUP, :] for h in range(high_count)]
        return jnp.concatenate(pieces, axis=1)

    for i in range(rows // (2 * GROUP)):
        r0 = i * (2 * rows_per_group)
        both = jnp.concatenate([group_rows(r0), group_rows(r0 + rows_per_group)], axis=0)
        table_ref[i * 2 * GROUP : (i + 1) * 2 * GROUP, :] = both.astype(jnp.bfloat16)


def multiply(table_ref, weight_ref, write):
    columns = weight_ref.shape[1]
    tile = min(TILE, columns)
    for c in range(0, columns, tile):
        at = slice(c, c + tile)
        write(at, jnp.dot(table_ref[...], weight_ref[:, at], preferred_element_type=jnp.float32))


def keys_scratch(rows):
    return pltpu.VMEM((rows + rows // 2, LANES), jnp.float32)


def start_loads(weight_hbm, tokens_hbm, column0, weight_ref, tokens_ref, sems):
    width, columns = weight_ref.shape
    part = width // LOAD_PARTS
    copies = []
    for i in range(LOAD_PARTS):
        rows = pl.ds(i * part, part)
        copies.append(
            pltpu.make_async_copy(weight_hbm.at[rows, pl.ds(column0, columns)], weight_ref.at[rows, :], sems.at[i])
        )
    copies.append(pltpu.make_async_copy(tokens_hbm.at[:, pl.ds(column0, columns)], tokens_ref, sems.at[LOAD_PARTS]))
    for copy in copies:
        copy.start()
    return copies


def multiply_loaded(copies, table_ref, weight_ref, tokens_ref):
    part = weight_ref.shape[0] // LOAD_PARTS
    total = None
    for i in range(LOAD_PARTS):
        copies[i].wait()
        at = slice(i * part, (i + 1) * part)
        product = jnp.dot(table_ref[:, at], weight_ref[at, :], preferred_element_type=jnp.float32)
        total = product if total is None else total + product
    copies[LOAD_PARTS].wait()
    return total - tokens_ref[...].astype(jnp.float32)


def begin_kernel(
    first_ref, ids_hbm, values_hbm, weight_hbm, tokens_hbm,
    weight_ref, table_ref, message_ref,
    ids_ref, values_ref, wide_ref, keys_ref, tokens_ref, sems,
):
    small = [
        pltpu.make_async_copy(ids_hbm, ids_ref, sems.at[LOAD_PARTS + 1]),
        pltpu.make_async_copy(values_hbm, values_ref, sems.at[LOAD_PARTS + 2]),
    ]
    for copy in small:
        copy.start()
    copies = start_loads(weight_hbm, tokens_hbm, 0, weight_ref, tokens_ref, sems)
    for copy in small:
        copy.wait()
    packed = pack(ids_ref[...], values_ref[...], wide_ref)
    columns = weight_ref.shape[1]
    message_ref[:, columns:] = packed.astype(message_ref.dtype)
    build_table(first_ref[0], packed, table_ref, keys_ref)
    total = multiply_loaded(copies, table_ref, weight_ref, tokens_ref)
    message_ref[:, :columns] = total.astype(message_ref.dtype)


def begin(first, ids, values, weight, tokens, columns):
    width = weight.shape[0]
    rows, active = ids.shape
    return pl.pallas_call(
        begin_kernel,
        in_specs=[IN_SMEM] + [IN_HBM] * 4,
        out_specs=[IN_VMEM] * 3,
        out_shape=[
            jax.ShapeDtypeStruct((width, columns), weight.dtype),
            jax.ShapeDtypeStruct((rows, width), jnp.bfloat16),
            jax.ShapeDtypeStruct((rows, columns + 2 * active), jnp.bfloat16),
        ],
        scratch_shapes=[
            pltpu.VMEM((active, rows), ids.dtype),
            pltpu.VMEM((active, rows), values.dtype),
            pltpu.VMEM((2 * rows, active), jnp.float32),
            keys_scratch(rows),
            pltpu.VMEM((rows, columns), tokens.dtype),
            pltpu.SemaphoreType.DMA((LOAD_PARTS + 3,)),
        ],
        compiler_params=params(),
        cost_estimate=cost(1 << 20),
        name="begin",
    )(first, in_hbm(ids.T), in_hbm(values.T), in_hbm(weight), in_hbm(tokens))


def second_kernel(column0, table_ref, weight_hbm, tokens_hbm, weight_ref, out_ref, tokens_ref, sems):
    copies = start_loads(weight_hbm, tokens_hbm, column0, weight_ref, tokens_ref, sems)
    out_ref[...] = multiply_loaded(copies, table_ref, weight_ref, tokens_ref).astype(out_ref.dtype)


def second(table, weight, tokens, column0, columns):
    width = weight.shape[0]
    rows = tokens.shape[0]
    return pl.pallas_call(
        functools.partial(second_kernel, column0),
        in_specs=[IN_VMEM, IN_HBM, IN_HBM],
        out_specs=[IN_VMEM] * 2,
        out_shape=[
            jax.ShapeDtypeStruct((width, columns), weight.dtype),
            jax.ShapeDtypeStruct((rows, columns), jnp.bfloat16),
        ],
        scratch_shapes=[
            pltpu.VMEM((rows, columns), tokens.dtype),
            pltpu.SemaphoreType.DMA((LOAD_PARTS + 1,)),
        ],
        compiler_params=params(),
        cost_estimate=cost(1 << 20),
        name="second",
    )(table, in_hbm(weight), in_hbm(tokens))


def step_kernel(column0, builds, last, *refs):
    if builds:
        first_ref, arrived_ref, weight_ref, bias_ref, table_ref, out_ref, keys_ref = refs
    else:
        table_ref, arrived_ref, weight_ref, bias_ref, out_ref = refs
    columns = weight_ref.shape[1]
    if builds:
        build_table(first_ref[0], arrived_ref[:, columns:].astype(jnp.float32), table_ref, keys_ref)
        if not last:
            out_ref[:, columns:] = arrived_ref[:, columns:]

    def write(at, product):
        total = product + arrived_ref[:, at].astype(jnp.float32)
        if last:
            total = total + bias_ref[:, column0 + at.start : column0 + at.stop]
        out_ref[:, at] = total.astype(out_ref.dtype)

    multiply(table_ref, weight_ref, write)


def step_a(first, arrived, weight, bias, last):
    width, columns = weight.shape
    rows = arrived.shape[0]
    return pl.pallas_call(
        functools.partial(step_kernel, 0, True, last),
        in_specs=[IN_SMEM] + [IN_VMEM] * 3,
        out_specs=[IN_VMEM] * 2,
        out_shape=[
            jax.ShapeDtypeStruct((rows, width), jnp.bfloat16),
            jax.ShapeDtypeStruct((rows, columns if last else arrived.shape[1]), jnp.bfloat16),
        ],
        scratch_shapes=[keys_scratch(rows)],
        compiler_params=params(),
        cost_estimate=cost(1 << 20),
        name="step_a",
    )(first, arrived, weight, bias)


def step_b(table, arrived, weight, bias, column0, last):
    return pl.pallas_call(
        functools.partial(step_kernel, column0, False, last),
        in_specs=[IN_VMEM] * 4,
        out_specs=IN_VMEM,
        out_shape=jax.ShapeDtypeStruct(arrived.shape, jnp.bfloat16),
        compiler_params=params(),
        cost_estimate=cost(1 << 20),
        name="step_b",
    )(table, arrived, weight, bias)


def grad_kernel(blocks, column0, tile, *refs):
    tables, errors = refs[:blocks], refs[blocks : 2 * blocks]
    error_out, grad_out, all_ref, made_ref, sems = refs[-5:]
    rows, columns = errors[0].shape
    width = tables[0].shape[1]
    at = pl.ds(column0, columns)
    copies = [pltpu.make_async_copy(errors[1], error_out.at[:, at], sems.at[width // tile])]
    copies[0].start()
    for b in range(blocks):
        all_ref[b * rows : (b + 1) * rows, :] = errors[b][...]
    for i, l in enumerate(range(0, width, tile)):
        table = jnp.concatenate([table_ref[:, l : l + tile] for table_ref in tables], axis=0)
        product = lax.dot_general(table, all_ref[...], (((0,), (0,)), ((), ())), preferred_element_type=jnp.float32)
        made_ref[l : l + tile, :] = product.astype(made_ref.dtype)
        copy = pltpu.make_async_copy(made_ref.at[pl.ds(l, tile), :], grad_out.at[pl.ds(l, tile), at], sems.at[i])
        copy.start()
        copies.append(copy)
    for copy in copies:
        copy.wait()


def grad_part(tables, errors, features, column0, previous, tile=256):
    width = tables[0].shape[1]
    rows, columns = errors[0].shape
    blocks = len(errors)
    in_specs = [IN_VMEM] * (2 * blocks)
    operands = [*tables, *errors]
    aliases = {}
    if previous is not None:
        aliases = {len(operands): 0, len(operands) + 1: 1}
        in_specs += [IN_HBM, IN_HBM]
        operands += previous
    return pl.pallas_call(
        functools.partial(grad_kernel, blocks, column0, tile),
        in_specs=in_specs,
        out_specs=[IN_HBM, IN_HBM],
        out_shape=[
            jax.ShapeDtypeStruct((rows, features), jnp.bfloat16),
            jax.ShapeDtypeStruct((width, features), jnp.bfloat16),
        ],
        scratch_shapes=[
            pltpu.VMEM((blocks * rows, columns), jnp.bfloat16),
            pltpu.VMEM((width, columns), jnp.bfloat16),
            pltpu.SemaphoreType.DMA((width // tile + 1,)),
        ],
        input_output_aliases=aliases,
        compiler_params=params(),
        cost_estimate=cost(1 << 20),
        name="grad",
    )(*operands)


def local(count, tokens, active_latent_index, latent_values, dec_bias, dec_weight):
    width, features = dec_weight.shape
    columns = features // 2
    first = (lax.axis_index("latent") * (width // LANES)).astype(jnp.int32).reshape(1)
    bias = dec_bias.reshape(1, features)

    def send(x):
        return lax.ppermute(x, "latent", ring_next(count))

    weight_a, own_table, a = begin(first, active_latent_index, latent_values, dec_weight, tokens, columns)
    weight_b, b = second(own_table, dec_weight, tokens, columns, columns)
    tables = [own_table]
    for k in range(1, count):
        last = k == count - 1
        table, a = step_a(first, send(a), weight_a, bias, last)
        b = step_b(table, send(b), weight_b, bias, columns, last)
        tables.append(table)
    errors_a, errors_b = [a], [b]
    for step in range(1, count):
        errors_a.append(send(errors_a[-1]))
        errors_b.append(send(errors_b[-1]))
    tables = [tables[-1]] + tables[:-1]
    made = grad_part(tables, errors_a, features, 0, None)
    made = grad_part(tables, errors_b, features, columns, made)
    return tuple(made)


def solution(mesh):
    in_specs = (
        P(("groups", "latent"), ("dp", "mp")),
        P(("groups", "latent"), None),
        P(("groups", "latent"), None),
        P(("groups", "dp", "mp")),
        P(("groups", "latent"), ("dp", "mp")),
    )
    out_specs = (P(("groups", "latent"), ("dp", "mp")), P(("groups", "latent"), ("dp", "mp")))
    body = functools.partial(local, mesh.shape["latent"])
    return jax.shard_map(body, mesh=mesh, in_specs=in_specs, out_specs=out_specs, check_vma=False)
```

```python
import functools

import jax
import jax.numpy as jnp
from jax import lax
from jax.experimental import pallas as pl
from jax.experimental.pallas import tpu as pltpu
from jax.sharding import PartitionSpec as P

LANES = 128
EXPONENT_BITS = (1, 2, 4, 8, 16, 32, 64)
GROUP = 8
TILE = 512
LOAD_PARTS = 8
VMEM_LIMIT = 24 * 1024 * 1024
IN_VMEM = pl.BlockSpec(memory_space=pltpu.VMEM)
IN_SMEM = pl.BlockSpec(memory_space=pltpu.SMEM)
IN_HBM = pl.BlockSpec(memory_space=pltpu.HBM)


def params():
    return pltpu.CompilerParams(vmem_limit_bytes=VMEM_LIMIT)


def in_hbm(array):
    return pltpu.with_memory_space_constraint(array, pltpu.HBM)


def cost(byte_count):
    return pl.CostEstimate(flops=0, bytes_accessed=byte_count, transcendentals=0)


def ring_order(count):
    return [0] + list(range(1, count, 2)) + list(range(count - 2 + count % 2, 0, -2))


def ring_next(count):
    order = ring_order(count)
    return [(order[i], order[(i + 1) % count]) for i in range(count)]


def pack(ids, values, wide_ref):
    active, rows = ids.shape
    high = lax.shift_right_logical(ids, 7)
    low = jnp.bitwise_and(ids, LANES - 1)
    coded = 1.0 + low.astype(jnp.float32) * (1.0 / LANES)
    for bit in EXPONENT_BITS:
        coded = jnp.where(jnp.bitwise_and(high, bit) != 0, coded * 2.0**bit, coded)
    coded = jnp.where(high >= LANES, -coded, coded)
    wide_ref[0:rows, :] = coded.T
    wide_ref[rows:, :] = values.astype(jnp.float32).T
    even = wide_ref[pl.ds(0, rows, stride=2), :]
    odd = wide_ref[pl.ds(1, rows, stride=2), :]
    return jnp.concatenate([even, odd], axis=1)


def unpack_ids(coded):
    rest = jnp.abs(coded)
    high = jnp.where(coded < 0, LANES, 0)
    for bit in reversed(EXPONENT_BITS):
        over = rest >= 2.0**bit
        rest = jnp.where(over, rest * 2.0**-bit, rest)
        high = high + jnp.where(over, bit, 0)
    return high, ((rest - 1.0) * LANES).astype(jnp.int32)


def build_table(first, packed, table_ref, keys_ref):
    rows, width = table_ref.shape
    half = rows // 2
    per_row = 2
    rows_per_group = GROUP // per_row
    high_count = width // LANES
    high, low = unpack_ids(packed[0:half, :])
    high = high - first
    row = lax.broadcasted_iota(jnp.int32, high.shape, 0)
    lane = lax.broadcasted_iota(jnp.int32, high.shape, 1)
    place = per_row * jnp.bitwise_and(row, rows_per_group - 1) + jnp.where(lane >= LANES // 2, 1, 0)
    inside = jnp.logical_and(high >= 0, high < high_count)
    key = jnp.where(inside, high * GROUP + place, -1)
    keys_ref[0:half, :] = key.astype(jnp.float32)
    keys_ref[half : 2 * half, :] = low.astype(jnp.float32)
    keys_ref[2 * half :, :] = packed[half:, :]
    tall = lax.broadcasted_iota(jnp.int32, (high_count * GROUP, LANES), 0).astype(jnp.float32).astype(jnp.bfloat16)
    wide = lax.broadcasted_iota(jnp.int32, (LANES, LANES), 0).astype(jnp.float32).astype(jnp.bfloat16)
    zero, one = jnp.zeros((), jnp.bfloat16), jnp.ones((), jnp.bfloat16)

    def group_rows(r0):
        left, right = [], []
        for r in range(r0, r0 + rows_per_group):
            key = keys_ref[r : r + 1, :].astype(jnp.bfloat16)
            low = keys_ref[half + r : half + r + 1, :].astype(jnp.bfloat16)
            value = keys_ref[2 * half + r : 2 * half + r + 1, :].astype(jnp.bfloat16)
            left.append(jnp.where(tall == key, value, zero))
            right.append(jnp.where(wide == low, one, zero))
        left = jnp.concatenate(left, axis=1)
        right = jnp.concatenate(right, axis=1)
        product = lax.dot_general(left, right, (((1,), (1,)), ((), ())), preferred_element_type=jnp.float32)
        pieces = [product[h * GROUP : (h + 1) * GROUP, :] for h in range(high_count)]
        return jnp.concatenate(pieces, axis=1)

    for i in range(rows // (2 * GROUP)):
        r0 = i * (2 * rows_per_group)
        both = jnp.concatenate([group_rows(r0), group_rows(r0 + rows_per_group)], axis=0)
        table_ref[i * 2 * GROUP : (i + 1) * 2 * GROUP, :] = both.astype(jnp.bfloat16)


def multiply(table_ref, weight_ref, write):
    columns = weight_ref.shape[1]
    tile = min(TILE, columns)
    for c in range(0, columns, tile):
        at = slice(c, c + tile)
        write(at, jnp.dot(table_ref[...], weight_ref[:, at], preferred_element_type=jnp.float32))


def keys_scratch(rows):
    return pltpu.VMEM((rows + rows // 2, LANES), jnp.float32)


def start_loads(weight_hbm, tokens_hbm, column0, weight_ref, tokens_ref, sems):
    width, columns = weight_ref.shape
    part = width // LOAD_PARTS
    copies = []
    for i in range(LOAD_PARTS):
        rows = pl.ds(i * part, part)
        copies.append(
            pltpu.make_async_copy(weight_hbm.at[rows, pl.ds(column0, columns)], weight_ref.at[rows, :], sems.at[i])
        )
    copies.append(pltpu.make_async_copy(tokens_hbm.at[:, pl.ds(column0, columns)], tokens_ref, sems.at[LOAD_PARTS]))
    for copy in copies:
        copy.start()
    return copies


def multiply_loaded(copies, table_ref, weight_ref, tokens_ref):
    part = weight_ref.shape[0] // LOAD_PARTS
    total = None
    for i in range(LOAD_PARTS):
        copies[i].wait()
        at = slice(i * part, (i + 1) * part)
        product = jnp.dot(table_ref[:, at], weight_ref[at, :], preferred_element_type=jnp.float32)
        total = product if total is None else total + product
    copies[LOAD_PARTS].wait()
    return total - tokens_ref[...].astype(jnp.float32)


def begin_kernel(
    first_ref, ids_hbm, values_hbm, weight_hbm, tokens_hbm,
    weight_ref, table_ref, message_ref,
    ids_ref, values_ref, wide_ref, keys_ref, tokens_ref, sems,
):
    small = [
        pltpu.make_async_copy(ids_hbm, ids_ref, sems.at[LOAD_PARTS + 1]),
        pltpu.make_async_copy(values_hbm, values_ref, sems.at[LOAD_PARTS + 2]),
    ]
    for copy in small:
        copy.start()
    copies = start_loads(weight_hbm, tokens_hbm, 0, weight_ref, tokens_ref, sems)
    for copy in small:
        copy.wait()
    packed = pack(ids_ref[...], values_ref[...], wide_ref)
    columns = weight_ref.shape[1]
    message_ref[:, columns:] = packed.astype(message_ref.dtype)
    build_table(first_ref[0], packed, table_ref, keys_ref)
    total = multiply_loaded(copies, table_ref, weight_ref, tokens_ref)
    message_ref[:, :columns] = total.astype(message_ref.dtype)


def begin(first, ids, values, weight, tokens, columns):
    width = weight.shape[0]
    rows, active = ids.shape
    return pl.pallas_call(
        begin_kernel,
        in_specs=[IN_SMEM] + [IN_HBM] * 4,
        out_specs=[IN_VMEM] * 3,
        out_shape=[
            jax.ShapeDtypeStruct((width, columns), weight.dtype),
            jax.ShapeDtypeStruct((rows, width), jnp.bfloat16),
            jax.ShapeDtypeStruct((rows, columns + 2 * active), jnp.bfloat16),
        ],
        scratch_shapes=[
            pltpu.VMEM((active, rows), ids.dtype),
            pltpu.VMEM((active, rows), values.dtype),
            pltpu.VMEM((2 * rows, active), jnp.float32),
            keys_scratch(rows),
            pltpu.VMEM((rows, columns), tokens.dtype),
            pltpu.SemaphoreType.DMA((LOAD_PARTS + 3,)),
        ],
        compiler_params=params(),
        cost_estimate=cost(1 << 20),
        name="begin",
    )(first, in_hbm(ids.T), in_hbm(values.T), in_hbm(weight), in_hbm(tokens))


def second_kernel(column0, table_ref, weight_hbm, tokens_hbm, weight_ref, out_ref, tokens_ref, sems):
    copies = start_loads(weight_hbm, tokens_hbm, column0, weight_ref, tokens_ref, sems)
    out_ref[...] = multiply_loaded(copies, table_ref, weight_ref, tokens_ref).astype(out_ref.dtype)


def second(table, weight, tokens, column0, columns):
    width = weight.shape[0]
    rows = tokens.shape[0]
    return pl.pallas_call(
        functools.partial(second_kernel, column0),
        in_specs=[IN_VMEM, IN_HBM, IN_HBM],
        out_specs=[IN_VMEM] * 2,
        out_shape=[
            jax.ShapeDtypeStruct((width, columns), weight.dtype),
            jax.ShapeDtypeStruct((rows, columns), jnp.bfloat16),
        ],
        scratch_shapes=[
            pltpu.VMEM((rows, columns), tokens.dtype),
            pltpu.SemaphoreType.DMA((LOAD_PARTS + 1,)),
        ],
        compiler_params=params(),
        cost_estimate=cost(1 << 20),
        name="second",
    )(table, in_hbm(weight), in_hbm(tokens))


def step_kernel(column0, builds, last, *refs):
    if builds:
        first_ref, arrived_ref, weight_ref, bias_ref, table_ref, out_ref, keys_ref = refs
    else:
        table_ref, arrived_ref, weight_ref, bias_ref, out_ref = refs
    columns = weight_ref.shape[1]
    if builds:
        build_table(first_ref[0], arrived_ref[:, columns:].astype(jnp.float32), table_ref, keys_ref)
        if not last:
            out_ref[:, columns:] = arrived_ref[:, columns:]

    def write(at, product):
        total = product + arrived_ref[:, at].astype(jnp.float32)
        if last:
            total = total + bias_ref[:, column0 + at.start : column0 + at.stop]
        out_ref[:, at] = total.astype(out_ref.dtype)

    multiply(table_ref, weight_ref, write)


def step_a(first, arrived, weight, bias, last):
    width, columns = weight.shape
    rows = arrived.shape[0]
    return pl.pallas_call(
        functools.partial(step_kernel, 0, True, last),
        in_specs=[IN_SMEM] + [IN_VMEM] * 3,
        out_specs=[IN_VMEM] * 2,
        out_shape=[
            jax.ShapeDtypeStruct((rows, width), jnp.bfloat16),
            jax.ShapeDtypeStruct((rows, columns if last else arrived.shape[1]), jnp.bfloat16),
        ],
        scratch_shapes=[keys_scratch(rows)],
        compiler_params=params(),
        cost_estimate=cost(1 << 20),
        name="step_a",
    )(first, arrived, weight, bias)


def step_b(table, arrived, weight, bias, column0, last):
    return pl.pallas_call(
        functools.partial(step_kernel, column0, False, last),
        in_specs=[IN_VMEM] * 4,
        out_specs=IN_VMEM,
        out_shape=jax.ShapeDtypeStruct(arrived.shape, jnp.bfloat16),
        compiler_params=params(),
        cost_estimate=cost(1 << 20),
        name="step_b",
    )(table, arrived, weight, bias)


def contract_tokens(tables, all_ref, at):
    table = jnp.concatenate([table_ref[:, at] for table_ref in tables], axis=0)
    return lax.dot_general(table, all_ref[...], (((0,), (0,)), ((), ())), preferred_element_type=jnp.float32)


def gather_errors(errors, all_ref):
    rows = errors[0].shape[0]
    for b, error_ref in enumerate(errors):
        all_ref[b * rows : (b + 1) * rows, :] = error_ref[...]


def early_kernel(blocks, tile, *refs):
    tables, errors, out_ref, all_ref = refs[:blocks], refs[blocks : 2 * blocks], refs[-2], refs[-1]
    gather_errors(errors, all_ref)
    for l in range(0, out_ref.shape[0], tile):
        at = slice(l, l + tile)
        out_ref[at, :] = contract_tokens(tables, all_ref, at)


def early_grad(tables, errors, tile=256):
    width = tables[0].shape[1]
    rows, columns = errors[0].shape
    blocks = len(errors)
    return pl.pallas_call(
        functools.partial(early_kernel, blocks, tile),
        in_specs=[IN_VMEM] * (2 * blocks),
        out_specs=IN_VMEM,
        out_shape=jax.ShapeDtypeStruct((width, columns), jnp.float32),
        scratch_shapes=[pltpu.VMEM((blocks * rows, columns), jnp.bfloat16)],
        compiler_params=params(),
        cost_estimate=cost(1 << 20),
        name="early_grad",
    )(*tables, *errors)


def grad_kernel(blocks, column0, tile, *refs):
    tables, errors, (own_ref, early_ref) = refs[:blocks], refs[blocks : 2 * blocks], refs[2 * blocks : 2 * blocks + 2]
    error_out, grad_out, all_ref, made_ref, sems = refs[-5:]
    rows, columns = errors[0].shape
    width = tables[0].shape[1]
    part = pl.ds(column0, columns)
    copies = [pltpu.make_async_copy(own_ref, error_out.at[:, part], sems.at[width // tile])]
    copies[0].start()
    gather_errors(errors, all_ref)
    for i, l in enumerate(range(0, width, tile)):
        at = slice(l, l + tile)
        product = contract_tokens(tables, all_ref, at) + early_ref[at, :]
        made_ref[at, :] = product.astype(made_ref.dtype)
        copy = pltpu.make_async_copy(made_ref.at[pl.ds(l, tile), :], grad_out.at[pl.ds(l, tile), part], sems.at[i])
        copy.start()
        copies.append(copy)
    for copy in copies:
        copy.wait()


def grad_part(tables, errors, own, early, features, column0, previous, tile=256):
    width = tables[0].shape[1]
    rows, columns = errors[0].shape
    blocks = len(errors)
    in_specs = [IN_VMEM] * (2 * blocks + 2)
    operands = [*tables, *errors, own, early]
    aliases = {}
    if previous is not None:
        aliases = {len(operands): 0, len(operands) + 1: 1}
        in_specs += [IN_HBM, IN_HBM]
        operands += previous
    return pl.pallas_call(
        functools.partial(grad_kernel, blocks, column0, tile),
        in_specs=in_specs,
        out_specs=[IN_HBM, IN_HBM],
        out_shape=[
            jax.ShapeDtypeStruct((rows, features), jnp.bfloat16),
            jax.ShapeDtypeStruct((width, features), jnp.bfloat16),
        ],
        scratch_shapes=[
            pltpu.VMEM((blocks * rows, columns), jnp.bfloat16),
            pltpu.VMEM((width, columns), jnp.bfloat16),
            pltpu.SemaphoreType.DMA((width // tile + 1,)),
        ],
        input_output_aliases=aliases,
        compiler_params=params(),
        cost_estimate=cost(1 << 20),
        name="grad",
    )(*operands)


def local(count, tokens, active_latent_index, latent_values, dec_bias, dec_weight):
    width, features = dec_weight.shape
    columns = features // 2
    first = (lax.axis_index("latent") * (width // LANES)).astype(jnp.int32).reshape(1)
    bias = dec_bias.reshape(1, features)

    def send(x):
        return lax.ppermute(x, "latent", ring_next(count))

    weight_a, own_table, a = begin(first, active_latent_index, latent_values, dec_weight, tokens, columns)
    weight_b, b = second(own_table, dec_weight, tokens, columns, columns)
    tables = [own_table]
    for k in range(1, count):
        last = k == count - 1
        table, a = step_a(first, send(a), weight_a, bias, last)
        b = step_b(table, send(b), weight_b, bias, columns, last)
        tables.append(table)
    errors = [[a], [b]]
    tables = [tables[-1]] + tables[:-1]
    split = max(1, count - 2)
    early = [None, None]
    for arrived in range(1, count):
        for c, chain in enumerate(errors):
            if arrived == count - 1:
                early[c] = early_grad(tables[:split], chain[:split])
                chain[-1], early[c] = lax.optimization_barrier((chain[-1], early[c]))
            chain.append(send(chain[-1]))
    made = None
    for chain, part, at in zip(errors, early, (0, columns)):
        made = grad_part(tables[split:], chain[split:], chain[1], part, features, at, made)
    return tuple(made)


def solution(mesh):
    in_specs = (
        P(("groups", "latent"), ("dp", "mp")),
        P(("groups", "latent"), None),
        P(("groups", "latent"), None),
        P(("groups", "dp", "mp")),
        P(("groups", "latent"), ("dp", "mp")),
    )
    out_specs = (P(("groups", "latent"), ("dp", "mp")), P(("groups", "latent"), ("dp", "mp")))
    body = functools.partial(local, mesh.shape["latent"])
    return jax.shard_map(body, mesh=mesh, in_specs=in_specs, out_specs=out_specs, check_vma=False)
```

```python
import functools

import jax
import jax.numpy as jnp
from jax import lax
from jax.experimental import pallas as pl
from jax.experimental.pallas import tpu as pltpu
from jax.sharding import PartitionSpec as P

LANES = 128
EXPONENT_BITS = (1, 2, 4, 8, 16, 32, 64)
GROUP = 8
TILE = 512
LOAD_PARTS = 4
VMEM_LIMIT = 24 * 1024 * 1024
IN_VMEM = pl.BlockSpec(memory_space=pltpu.VMEM)
IN_SMEM = pl.BlockSpec(memory_space=pltpu.SMEM)
IN_HBM = pl.BlockSpec(memory_space=pltpu.HBM)


def params():
    return pltpu.CompilerParams(vmem_limit_bytes=VMEM_LIMIT)


def in_hbm(array):
    return pltpu.with_memory_space_constraint(array, pltpu.HBM)


def cost(byte_count):
    return pl.CostEstimate(flops=0, bytes_accessed=byte_count, transcendentals=0)


def ring_order(count):
    return [0] + list(range(2, count, 2)) + list(range(count - 1 - count % 2, 0, -2))


def ring_next(count):
    order = ring_order(count)
    return [(order[i], order[(i + 1) % count]) for i in range(count)]


def pack(ids, values, wide_ref):
    active, rows = ids.shape
    high = lax.shift_right_logical(ids, 7)
    low = jnp.bitwise_and(ids, LANES - 1)
    coded = 1.0 + low.astype(jnp.float32) * (1.0 / LANES)
    for bit in EXPONENT_BITS:
        coded = jnp.where(jnp.bitwise_and(high, bit) != 0, coded * 2.0**bit, coded)
    coded = jnp.where(high >= LANES, -coded, coded)
    wide_ref[0:rows, :] = coded.T
    wide_ref[rows:, :] = values.astype(jnp.float32).T
    even = wide_ref[pl.ds(0, rows, stride=2), :]
    odd = wide_ref[pl.ds(1, rows, stride=2), :]
    return jnp.concatenate([even, odd], axis=1)


def unpack_ids(coded):
    rest = jnp.abs(coded)
    high = jnp.where(coded < 0, LANES, 0)
    for bit in reversed(EXPONENT_BITS):
        over = rest >= 2.0**bit
        rest = jnp.where(over, rest * 2.0**-bit, rest)
        high = high + jnp.where(over, bit, 0)
    return high, ((rest - 1.0) * LANES).astype(jnp.int32)


def build_table(first, packed, table_ref, keys_ref):
    rows, width = table_ref.shape
    half = rows // 2
    per_row = 2
    rows_per_group = GROUP // per_row
    high_count = width // LANES
    high, low = unpack_ids(packed[0:half, :])
    high = high - first
    row = lax.broadcasted_iota(jnp.int32, high.shape, 0)
    lane = lax.broadcasted_iota(jnp.int32, high.shape, 1)
    place = per_row * jnp.bitwise_and(row, rows_per_group - 1) + jnp.where(lane >= LANES // 2, 1, 0)
    inside = jnp.logical_and(high >= 0, high < high_count)
    key = jnp.where(inside, high * GROUP + place, -1)
    keys_ref[0:half, :] = key.astype(jnp.float32)
    keys_ref[half : 2 * half, :] = low.astype(jnp.float32)
    keys_ref[2 * half :, :] = packed[half:, :]
    tall = lax.broadcasted_iota(jnp.int32, (high_count * GROUP, LANES), 0).astype(jnp.float32).astype(jnp.bfloat16)
    wide = lax.broadcasted_iota(jnp.int32, (LANES, LANES), 0).astype(jnp.float32).astype(jnp.bfloat16)
    zero, one = jnp.zeros((), jnp.bfloat16), jnp.ones((), jnp.bfloat16)

    def group_rows(r0):
        left, right = [], []
        for r in range(r0, r0 + rows_per_group):
            key = keys_ref[r : r + 1, :].astype(jnp.bfloat16)
            low = keys_ref[half + r : half + r + 1, :].astype(jnp.bfloat16)
            value = keys_ref[2 * half + r : 2 * half + r + 1, :].astype(jnp.bfloat16)
            left.append(jnp.where(tall == key, value, zero))
            right.append(jnp.where(wide == low, one, zero))
        left = jnp.concatenate(left, axis=1)
        right = jnp.concatenate(right, axis=1)
        product = lax.dot_general(left, right, (((1,), (1,)), ((), ())), preferred_element_type=jnp.float32)
        pieces = [product[h * GROUP : (h + 1) * GROUP, :] for h in range(high_count)]
        return jnp.concatenate(pieces, axis=1)

    for i in range(rows // (2 * GROUP)):
        r0 = i * (2 * rows_per_group)
        both = jnp.concatenate([group_rows(r0), group_rows(r0 + rows_per_group)], axis=0)
        table_ref[i * 2 * GROUP : (i + 1) * 2 * GROUP, :] = both.astype(jnp.bfloat16)


def multiply(table_ref, weight_ref, write):
    columns = weight_ref.shape[1]
    tile = min(TILE, columns)
    for c in range(0, columns, tile):
        at = slice(c, c + tile)
        write(at, jnp.dot(table_ref[...], weight_ref[:, at], preferred_element_type=jnp.float32))


def keys_scratch(rows):
    return pltpu.VMEM((rows + rows // 2, LANES), jnp.float32)


def start_loads(weight_hbm, tokens_hbm, column0, weight_ref, tokens_ref, sems):
    width, columns = weight_ref.shape
    part = width // LOAD_PARTS
    copies = []
    for i in range(LOAD_PARTS):
        rows = pl.ds(i * part, part)
        copies.append(
            pltpu.make_async_copy(weight_hbm.at[rows, pl.ds(column0, columns)], weight_ref.at[rows, :], sems.at[i])
        )
    copies.append(pltpu.make_async_copy(tokens_hbm.at[:, pl.ds(column0, columns)], tokens_ref, sems.at[LOAD_PARTS]))
    for copy in copies:
        copy.start()
    return copies


def multiply_loaded(copies, table_ref, weight_ref, tokens_ref):
    part = weight_ref.shape[0] // LOAD_PARTS
    total = None
    for i in range(LOAD_PARTS):
        copies[i].wait()
        at = slice(i * part, (i + 1) * part)
        product = jnp.dot(table_ref[:, at], weight_ref[at, :], preferred_element_type=jnp.float32)
        total = product if total is None else total + product
    copies[LOAD_PARTS].wait()
    return total - tokens_ref[...].astype(jnp.float32)


def begin_kernel(
    first_ref, ids_hbm, values_hbm, weight_hbm, tokens_hbm,
    weight_ref, table_ref, message_ref,
    ids_ref, values_ref, wide_ref, keys_ref, tokens_ref, sems,
):
    small = [
        pltpu.make_async_copy(ids_hbm, ids_ref, sems.at[LOAD_PARTS + 1]),
        pltpu.make_async_copy(values_hbm, values_ref, sems.at[LOAD_PARTS + 2]),
    ]
    for copy in small:
        copy.start()
    copies = start_loads(weight_hbm, tokens_hbm, 0, weight_ref, tokens_ref, sems)
    for copy in small:
        copy.wait()
    packed = pack(ids_ref[...], values_ref[...], wide_ref)
    columns = weight_ref.shape[1]
    message_ref[:, columns:] = packed.astype(message_ref.dtype)
    build_table(first_ref[0], packed, table_ref, keys_ref)
    total = multiply_loaded(copies, table_ref, weight_ref, tokens_ref)
    message_ref[:, :columns] = total.astype(message_ref.dtype)


def begin(first, ids, values, weight, tokens, columns):
    width = weight.shape[0]
    rows, active = ids.shape
    return pl.pallas_call(
        begin_kernel,
        in_specs=[IN_SMEM] + [IN_HBM] * 4,
        out_specs=[IN_VMEM] * 3,
        out_shape=[
            jax.ShapeDtypeStruct((width, columns), weight.dtype),
            jax.ShapeDtypeStruct((rows, width), jnp.bfloat16),
            jax.ShapeDtypeStruct((rows, columns + 2 * active), jnp.bfloat16),
        ],
        scratch_shapes=[
            pltpu.VMEM((active, rows), ids.dtype),
            pltpu.VMEM((active, rows), values.dtype),
            pltpu.VMEM((2 * rows, active), jnp.float32),
            keys_scratch(rows),
            pltpu.VMEM((rows, columns), tokens.dtype),
            pltpu.SemaphoreType.DMA((LOAD_PARTS + 3,)),
        ],
        compiler_params=params(),
        cost_estimate=cost(1 << 20),
        name="begin",
    )(first, in_hbm(ids.T), in_hbm(values.T), in_hbm(weight), in_hbm(tokens))


def second_kernel(column0, table_ref, weight_hbm, tokens_hbm, weight_ref, out_ref, tokens_ref, sems):
    copies = start_loads(weight_hbm, tokens_hbm, column0, weight_ref, tokens_ref, sems)
    out_ref[...] = multiply_loaded(copies, table_ref, weight_ref, tokens_ref).astype(out_ref.dtype)


def second(table, weight, tokens, column0, columns):
    width = weight.shape[0]
    rows = tokens.shape[0]
    return pl.pallas_call(
        functools.partial(second_kernel, column0),
        in_specs=[IN_VMEM, IN_HBM, IN_HBM],
        out_specs=[IN_VMEM] * 2,
        out_shape=[
            jax.ShapeDtypeStruct((width, columns), weight.dtype),
            jax.ShapeDtypeStruct((rows, columns), jnp.bfloat16),
        ],
        scratch_shapes=[
            pltpu.VMEM((rows, columns), tokens.dtype),
            pltpu.SemaphoreType.DMA((LOAD_PARTS + 1,)),
        ],
        compiler_params=params(),
        cost_estimate=cost(1 << 20),
        name="second",
    )(table, in_hbm(weight), in_hbm(tokens))


def step_kernel(column0, builds, last, *refs):
    if builds:
        first_ref, arrived_ref, weight_ref, bias_ref, table_ref, out_ref, keys_ref = refs
    else:
        table_ref, arrived_ref, weight_ref, bias_ref, out_ref = refs
    columns = weight_ref.shape[1]
    if builds:
        build_table(first_ref[0], arrived_ref[:, columns:].astype(jnp.float32), table_ref, keys_ref)
        if not last:
            out_ref[:, columns:] = arrived_ref[:, columns:]

    def write(at, product):
        total = product + arrived_ref[:, at].astype(jnp.float32)
        if last:
            total = total + bias_ref[:, column0 + at.start : column0 + at.stop]
        out_ref[:, at] = total.astype(out_ref.dtype)

    multiply(table_ref, weight_ref, write)


def step_a(first, arrived, weight, bias, last):
    width, columns = weight.shape
    rows = arrived.shape[0]
    return pl.pallas_call(
        functools.partial(step_kernel, 0, True, last),
        in_specs=[IN_SMEM] + [IN_VMEM] * 3,
        out_specs=[IN_VMEM] * 2,
        out_shape=[
            jax.ShapeDtypeStruct((rows, width), jnp.bfloat16),
            jax.ShapeDtypeStruct((rows, columns if last else arrived.shape[1]), jnp.bfloat16),
        ],
        scratch_shapes=[keys_scratch(rows)],
        compiler_params=params(),
        cost_estimate=cost(1 << 20),
        name="step_a",
    )(first, arrived, weight, bias)


def step_b(table, arrived, weight, bias, column0, last):
    return pl.pallas_call(
        functools.partial(step_kernel, column0, False, last),
        in_specs=[IN_VMEM] * 4,
        out_specs=IN_VMEM,
        out_shape=jax.ShapeDtypeStruct(arrived.shape, jnp.bfloat16),
        compiler_params=params(),
        cost_estimate=cost(1 << 20),
        name="step_b",
    )(table, arrived, weight, bias)


def contract_tokens(tables, all_ref, at):
    table = jnp.concatenate([table_ref[:, at] for table_ref in tables], axis=0)
    return lax.dot_general(table, all_ref[...], (((0,), (0,)), ((), ())), preferred_element_type=jnp.float32)


def gather_errors(errors, all_ref):
    rows = errors[0].shape[0]
    for b, error_ref in enumerate(errors):
        all_ref[b * rows : (b + 1) * rows, :] = error_ref[...]


def early_kernel(blocks, tile, *refs):
    tables, errors, out_ref, all_ref = refs[:blocks], refs[blocks : 2 * blocks], refs[-2], refs[-1]
    gather_errors(errors, all_ref)
    for l in range(0, out_ref.shape[0], tile):
        at = slice(l, l + tile)
        out_ref[at, :] = contract_tokens(tables, all_ref, at)


def early_grad(tables, errors, tile=256):
    width = tables[0].shape[1]
    rows, columns = errors[0].shape
    blocks = len(errors)
    return pl.pallas_call(
        functools.partial(early_kernel, blocks, tile),
        in_specs=[IN_VMEM] * (2 * blocks),
        out_specs=IN_VMEM,
        out_shape=jax.ShapeDtypeStruct((width, columns), jnp.float32),
        scratch_shapes=[pltpu.VMEM((blocks * rows, columns), jnp.bfloat16)],
        compiler_params=params(),
        cost_estimate=cost(1 << 20),
        name="early_grad",
    )(*tables, *errors)


def grad_kernel(blocks, column0, tile, *refs):
    tables, errors, (own_ref, early_ref) = refs[:blocks], refs[blocks : 2 * blocks], refs[2 * blocks : 2 * blocks + 2]
    error_out, grad_out, all_ref, made_ref, sems = refs[-5:]
    rows, columns = errors[0].shape
    width = tables[0].shape[1]
    part = pl.ds(column0, columns)
    copies = [pltpu.make_async_copy(own_ref, error_out.at[:, part], sems.at[width // tile])]
    copies[0].start()
    gather_errors(errors, all_ref)
    for i, l in enumerate(range(0, width, tile)):
        at = slice(l, l + tile)
        product = contract_tokens(tables, all_ref, at) + early_ref[at, :]
        made_ref[at, :] = product.astype(made_ref.dtype)
        copy = pltpu.make_async_copy(made_ref.at[pl.ds(l, tile), :], grad_out.at[pl.ds(l, tile), part], sems.at[i])
        copy.start()
        copies.append(copy)
    for copy in copies:
        copy.wait()


def grad_part(tables, errors, own, early, features, column0, previous, tile=256):
    width = tables[0].shape[1]
    rows, columns = errors[0].shape
    blocks = len(errors)
    in_specs = [IN_VMEM] * (2 * blocks + 2)
    operands = [*tables, *errors, own, early]
    aliases = {}
    if previous is not None:
        aliases = {len(operands): 0, len(operands) + 1: 1}
        in_specs += [IN_HBM, IN_HBM]
        operands += previous
    return pl.pallas_call(
        functools.partial(grad_kernel, blocks, column0, tile),
        in_specs=in_specs,
        out_specs=[IN_HBM, IN_HBM],
        out_shape=[
            jax.ShapeDtypeStruct((rows, features), jnp.bfloat16),
            jax.ShapeDtypeStruct((width, features), jnp.bfloat16),
        ],
        scratch_shapes=[
            pltpu.VMEM((blocks * rows, columns), jnp.bfloat16),
            pltpu.VMEM((width, columns), jnp.bfloat16),
            pltpu.SemaphoreType.DMA((width // tile + 1,)),
        ],
        input_output_aliases=aliases,
        compiler_params=params(),
        cost_estimate=cost(1 << 20),
        name="grad",
    )(*operands)


def local(count, tokens, active_latent_index, latent_values, dec_bias, dec_weight):
    width, features = dec_weight.shape
    columns = features // 2
    first = (lax.axis_index("latent") * (width // LANES)).astype(jnp.int32).reshape(1)
    bias = dec_bias.reshape(1, features)

    def send(x):
        return lax.ppermute(x, "latent", ring_next(count))

    weight_a, own_table, a = begin(first, active_latent_index, latent_values, dec_weight, tokens, columns)
    weight_b, b = second(own_table, dec_weight, tokens, columns, columns)
    tables = [own_table]
    for k in range(1, count):
        last = k == count - 1
        table, a = step_a(first, send(a), weight_a, bias, last)
        b = step_b(table, send(b), weight_b, bias, columns, last)
        tables.append(table)
    errors = [[a], [b]]
    tables = [tables[-1]] + tables[:-1]
    split = max(1, count - 2)
    early = [None, None]
    for arrived in range(1, count):
        for c, chain in enumerate(errors):
            if arrived == count - 1:
                early[c] = early_grad(tables[:split], chain[:split])
                chain[-1], early[c] = lax.optimization_barrier((chain[-1], early[c]))
            chain.append(send(chain[-1]))
    made = None
    for chain, part, at in zip(errors, early, (0, columns)):
        made = grad_part(tables[split:], chain[split:], chain[1], part, features, at, made)
    return tuple(made)


def solution(mesh):
    in_specs = (
        P(("groups", "latent"), ("dp", "mp")),
        P(("groups", "latent"), None),
        P(("groups", "latent"), None),
        P(("groups", "dp", "mp")),
        P(("groups", "latent"), ("dp", "mp")),
    )
    out_specs = (P(("groups", "latent"), ("dp", "mp")), P(("groups", "latent"), ("dp", "mp")))
    body = functools.partial(local, mesh.shape["latent"])
    return jax.shard_map(body, mesh=mesh, in_specs=in_specs, out_specs=out_specs, check_vma=False)
```

```python
import functools

import jax
import jax.numpy as jnp
from jax import lax
from jax.experimental import pallas as pl
from jax.experimental.pallas import tpu as pltpu
from jax.sharding import PartitionSpec as P

LANES = 128
EXPONENT_BITS = (1, 2, 4, 8, 16, 32, 64)
GROUP = 8
TILE = 512
LOAD_PARTS = 4
VMEM_LIMIT = 24 * 1024 * 1024
IN_VMEM = pl.BlockSpec(memory_space=pltpu.VMEM)
IN_SMEM = pl.BlockSpec(memory_space=pltpu.SMEM)
IN_HBM = pl.BlockSpec(memory_space=pltpu.HBM)


def params():
    return pltpu.CompilerParams(vmem_limit_bytes=VMEM_LIMIT)


def in_hbm(array):
    return pltpu.with_memory_space_constraint(array, pltpu.HBM)


def cost(byte_count):
    return pl.CostEstimate(flops=0, bytes_accessed=byte_count, transcendentals=0)


def ring_order(count):
    return [0] + list(range(2, count, 2)) + list(range(count - 1 - count % 2, 0, -2))


def ring_next(count):
    order = ring_order(count)
    return [(order[i], order[(i + 1) % count]) for i in range(count)]


def pack(ids, values, wide_ref):
    active, rows = ids.shape
    high = lax.shift_right_logical(ids, 7)
    low = jnp.bitwise_and(ids, LANES - 1)
    coded = 1.0 + low.astype(jnp.float32) * (1.0 / LANES)
    for bit in EXPONENT_BITS:
        coded = jnp.where(jnp.bitwise_and(high, bit) != 0, coded * 2.0**bit, coded)
    coded = jnp.where(high >= LANES, -coded, coded)
    wide_ref[0:rows, :] = coded.T
    wide_ref[rows:, :] = values.astype(jnp.float32).T
    even = wide_ref[pl.ds(0, rows, stride=2), :]
    odd = wide_ref[pl.ds(1, rows, stride=2), :]
    return jnp.concatenate([even, odd], axis=1)


def unpack_ids(coded):
    rest = jnp.abs(coded)
    high = jnp.where(coded < 0, LANES, 0)
    for bit in reversed(EXPONENT_BITS):
        over = rest >= 2.0**bit
        rest = jnp.where(over, rest * 2.0**-bit, rest)
        high = high + jnp.where(over, bit, 0)
    return high, ((rest - 1.0) * LANES).astype(jnp.int32)


def build_table(first, packed, table_ref, keys_ref):
    rows, width = table_ref.shape
    half = rows // 2
    per_row = 2
    rows_per_group = GROUP // per_row
    high_count = width // LANES
    high, low = unpack_ids(packed[0:half, :])
    high = high - first
    row = lax.broadcasted_iota(jnp.int32, high.shape, 0)
    lane = lax.broadcasted_iota(jnp.int32, high.shape, 1)
    place = per_row * jnp.bitwise_and(row, rows_per_group - 1) + jnp.where(lane >= LANES // 2, 1, 0)
    inside = jnp.logical_and(high >= 0, high < high_count)
    key = jnp.where(inside, high * GROUP + place, -1)
    keys_ref[0:half, :] = key.astype(jnp.float32)
    keys_ref[half : 2 * half, :] = low.astype(jnp.float32)
    keys_ref[2 * half :, :] = packed[half:, :]
    tall = lax.broadcasted_iota(jnp.int32, (high_count * GROUP, LANES), 0).astype(jnp.float32).astype(jnp.bfloat16)
    wide = lax.broadcasted_iota(jnp.int32, (LANES, LANES), 0).astype(jnp.float32).astype(jnp.bfloat16)
    zero, one = jnp.zeros((), jnp.bfloat16), jnp.ones((), jnp.bfloat16)

    def group_rows(r0):
        left, right = [], []
        for r in range(r0, r0 + rows_per_group):
            key = keys_ref[r : r + 1, :].astype(jnp.bfloat16)
            low = keys_ref[half + r : half + r + 1, :].astype(jnp.bfloat16)
            value = keys_ref[2 * half + r : 2 * half + r + 1, :].astype(jnp.bfloat16)
            left.append(jnp.where(tall == key, value, zero))
            right.append(jnp.where(wide == low, one, zero))
        left = jnp.concatenate(left, axis=1)
        right = jnp.concatenate(right, axis=1)
        product = lax.dot_general(left, right, (((1,), (1,)), ((), ())), preferred_element_type=jnp.float32)
        pieces = [product[h * GROUP : (h + 1) * GROUP, :] for h in range(high_count)]
        return jnp.concatenate(pieces, axis=1)

    for i in range(rows // (2 * GROUP)):
        r0 = i * (2 * rows_per_group)
        both = jnp.concatenate([group_rows(r0), group_rows(r0 + rows_per_group)], axis=0)
        table_ref[i * 2 * GROUP : (i + 1) * 2 * GROUP, :] = both.astype(jnp.bfloat16)


def multiply(table_ref, weight_ref, write):
    columns = weight_ref.shape[1]
    tile = min(TILE, columns)
    for c in range(0, columns, tile):
        at = slice(c, c + tile)
        write(at, jnp.dot(table_ref[...], weight_ref[:, at], preferred_element_type=jnp.float32))


def keys_scratch(rows):
    return pltpu.VMEM((rows + rows // 2, LANES), jnp.float32)


def start_loads(weight_hbm, tokens_hbm, column0, weight_ref, tokens_ref, sems):
    width, columns = weight_ref.shape
    part = width // LOAD_PARTS
    copies = []
    for i in range(LOAD_PARTS):
        rows = pl.ds(i * part, part)
        copies.append(
            pltpu.make_async_copy(weight_hbm.at[rows, pl.ds(column0, columns)], weight_ref.at[rows, :], sems.at[i])
        )
    copies.append(pltpu.make_async_copy(tokens_hbm.at[:, pl.ds(column0, columns)], tokens_ref, sems.at[LOAD_PARTS]))
    for copy in copies:
        copy.start()
    return copies


def multiply_loaded(copies, table_ref, weight_ref, tokens_ref):
    part = weight_ref.shape[0] // LOAD_PARTS
    total = None
    for i in range(LOAD_PARTS):
        copies[i].wait()
        at = slice(i * part, (i + 1) * part)
        product = jnp.dot(table_ref[:, at], weight_ref[at, :], preferred_element_type=jnp.float32)
        total = product if total is None else total + product
    copies[LOAD_PARTS].wait()
    return total - tokens_ref[...].astype(jnp.float32)


def begin_kernel(
    first_ref, ids_hbm, values_hbm, weight_hbm, tokens_hbm,
    weight_ref, table_ref, message_ref,
    ids_ref, values_ref, wide_ref, keys_ref, tokens_ref, sems,
):
    small = [
        pltpu.make_async_copy(ids_hbm, ids_ref, sems.at[LOAD_PARTS + 1]),
        pltpu.make_async_copy(values_hbm, values_ref, sems.at[LOAD_PARTS + 2]),
    ]
    for copy in small:
        copy.start()
    copies = start_loads(weight_hbm, tokens_hbm, 0, weight_ref, tokens_ref, sems)
    for copy in small:
        copy.wait()
    packed = pack(ids_ref[...], values_ref[...], wide_ref)
    columns = weight_ref.shape[1]
    message_ref[:, columns:] = packed.astype(message_ref.dtype)
    build_table(first_ref[0], packed, table_ref, keys_ref)
    total = multiply_loaded(copies, table_ref, weight_ref, tokens_ref)
    message_ref[:, :columns] = total.astype(message_ref.dtype)


def begin(first, ids, values, weight, tokens, columns):
    width = weight.shape[0]
    rows, active = ids.shape
    return pl.pallas_call(
        begin_kernel,
        in_specs=[IN_SMEM] + [IN_HBM] * 4,
        out_specs=[IN_VMEM] * 3,
        out_shape=[
            jax.ShapeDtypeStruct((width, columns), weight.dtype),
            jax.ShapeDtypeStruct((rows, width), jnp.bfloat16),
            jax.ShapeDtypeStruct((rows, columns + 2 * active), jnp.bfloat16),
        ],
        scratch_shapes=[
            pltpu.VMEM((active, rows), ids.dtype),
            pltpu.VMEM((active, rows), values.dtype),
            pltpu.VMEM((2 * rows, active), jnp.float32),
            keys_scratch(rows),
            pltpu.VMEM((rows, columns), tokens.dtype),
            pltpu.SemaphoreType.DMA((LOAD_PARTS + 3,)),
        ],
        compiler_params=params(),
        cost_estimate=cost(1 << 20),
        name="begin",
    )(first, in_hbm(ids.T), in_hbm(values.T), in_hbm(weight), in_hbm(tokens))


def second_kernel(column0, table_ref, weight_hbm, tokens_hbm, weight_ref, out_ref, tokens_ref, sems):
    copies = start_loads(weight_hbm, tokens_hbm, column0, weight_ref, tokens_ref, sems)
    out_ref[...] = multiply_loaded(copies, table_ref, weight_ref, tokens_ref).astype(out_ref.dtype)


def second(table, weight, tokens, column0, columns):
    width = weight.shape[0]
    rows = tokens.shape[0]
    return pl.pallas_call(
        functools.partial(second_kernel, column0),
        in_specs=[IN_VMEM, IN_HBM, IN_HBM],
        out_specs=[IN_VMEM] * 2,
        out_shape=[
            jax.ShapeDtypeStruct((width, columns), weight.dtype),
            jax.ShapeDtypeStruct((rows, columns), jnp.bfloat16),
        ],
        scratch_shapes=[
            pltpu.VMEM((rows, columns), tokens.dtype),
            pltpu.SemaphoreType.DMA((LOAD_PARTS + 1,)),
        ],
        compiler_params=params(),
        cost_estimate=cost(1 << 20),
        name="second",
    )(table, in_hbm(weight), in_hbm(tokens))


def step_kernel(last, first_ref, arrived_ref, weight_ref, bias_ref, table_ref, out_ref, keys_ref):
    columns = weight_ref.shape[1]
    build_table(first_ref[0], arrived_ref[:, columns:].astype(jnp.float32), table_ref, keys_ref)
    if not last:
        out_ref[:, columns:] = arrived_ref[:, columns:]

    def write(at, product):
        total = product + arrived_ref[:, at].astype(jnp.float32)
        if last:
            total = total + bias_ref[:, at]
        out_ref[:, at] = total.astype(out_ref.dtype)

    multiply(table_ref, weight_ref, write)


def step_a(first, arrived, weight, bias, last):
    width, columns = weight.shape
    rows = arrived.shape[0]
    return pl.pallas_call(
        functools.partial(step_kernel, last),
        in_specs=[IN_SMEM] + [IN_VMEM] * 3,
        out_specs=[IN_VMEM] * 2,
        out_shape=[
            jax.ShapeDtypeStruct((rows, width), jnp.bfloat16),
            jax.ShapeDtypeStruct((rows, columns if last else arrived.shape[1]), jnp.bfloat16),
        ],
        scratch_shapes=[keys_scratch(rows)],
        compiler_params=params(),
        cost_estimate=cost(1 << 20),
        name="step_a",
    )(first, arrived, weight, bias)


def multiply_kernel(table_ref, weight_ref, out_ref):
    def write(at, product):
        out_ref[:, at] = product

    multiply(table_ref, weight_ref, write)


def add_kernel(column0, last, part_ref, arrived_ref, bias_ref, out_ref):
    total = part_ref[...] + arrived_ref[...].astype(jnp.float32)
    if last:
        total = total + bias_ref[:, column0 : column0 + part_ref.shape[1]]
    out_ref[...] = total.astype(out_ref.dtype)


def step_b(table, arrived, weight, bias, column0, last):
    shape = arrived.shape
    part = pl.pallas_call(
        multiply_kernel,
        in_specs=[IN_VMEM] * 2,
        out_specs=IN_VMEM,
        out_shape=jax.ShapeDtypeStruct(shape, jnp.float32),
        compiler_params=params(),
        cost_estimate=cost(1 << 20),
        name="multiply",
    )(table, weight)
    return pl.pallas_call(
        functools.partial(add_kernel, column0, last),
        in_specs=[IN_VMEM] * 3,
        out_specs=IN_VMEM,
        out_shape=jax.ShapeDtypeStruct(shape, jnp.bfloat16),
        compiler_params=params(),
        cost_estimate=cost(1 << 20),
        name="add",
    )(part, arrived, bias)


def contract_tokens(tables, all_ref, at):
    table = jnp.concatenate([table_ref[:, at] for table_ref in tables], axis=0)
    return lax.dot_general(table, all_ref[...], (((0,), (0,)), ((), ())), preferred_element_type=jnp.float32)


def gather_errors(errors, all_ref):
    rows = errors[0].shape[0]
    for b, error_ref in enumerate(errors):
        all_ref[b * rows : (b + 1) * rows, :] = error_ref[...]


def early_kernel(blocks, tile, *refs):
    tables, errors, out_ref, all_ref = refs[:blocks], refs[blocks : 2 * blocks], refs[-2], refs[-1]
    gather_errors(errors, all_ref)
    for l in range(0, out_ref.shape[0], tile):
        at = slice(l, l + tile)
        out_ref[at, :] = contract_tokens(tables, all_ref, at)


def early_grad(tables, errors, tile=256):
    width = tables[0].shape[1]
    rows, columns = errors[0].shape
    blocks = len(errors)
    return pl.pallas_call(
        functools.partial(early_kernel, blocks, tile),
        in_specs=[IN_VMEM] * (2 * blocks),
        out_specs=IN_VMEM,
        out_shape=jax.ShapeDtypeStruct((width, columns), jnp.float32),
        scratch_shapes=[pltpu.VMEM((blocks * rows, columns), jnp.bfloat16)],
        compiler_params=params(),
        cost_estimate=cost(1 << 20),
        name="early_grad",
    )(*tables, *errors)


def grad_kernel(blocks, column0, tile, *refs):
    tables, errors, (own_ref, early_ref) = refs[:blocks], refs[blocks : 2 * blocks], refs[2 * blocks : 2 * blocks + 2]
    error_out, grad_out, all_ref, made_ref, sems = refs[-5:]
    rows, columns = errors[0].shape
    width = tables[0].shape[1]
    part = pl.ds(column0, columns)
    copies = [pltpu.make_async_copy(own_ref, error_out.at[:, part], sems.at[width // tile])]
    copies[0].start()
    gather_errors(errors, all_ref)
    for i, l in enumerate(range(0, width, tile)):
        at = slice(l, l + tile)
        product = contract_tokens(tables, all_ref, at) + early_ref[at, :]
        made_ref[at, :] = product.astype(made_ref.dtype)
        copy = pltpu.make_async_copy(made_ref.at[pl.ds(l, tile), :], grad_out.at[pl.ds(l, tile), part], sems.at[i])
        copy.start()
        copies.append(copy)
    for copy in copies:
        copy.wait()


def grad_part(tables, errors, own, early, features, column0, previous, tile=256):
    width = tables[0].shape[1]
    rows, columns = errors[0].shape
    blocks = len(errors)
    in_specs = [IN_VMEM] * (2 * blocks + 2)
    operands = [*tables, *errors, own, early]
    aliases = {}
    if previous is not None:
        aliases = {len(operands): 0, len(operands) + 1: 1}
        in_specs += [IN_HBM, IN_HBM]
        operands += previous
    return pl.pallas_call(
        functools.partial(grad_kernel, blocks, column0, tile),
        in_specs=in_specs,
        out_specs=[IN_HBM, IN_HBM],
        out_shape=[
            jax.ShapeDtypeStruct((rows, features), jnp.bfloat16),
            jax.ShapeDtypeStruct((width, features), jnp.bfloat16),
        ],
        scratch_shapes=[
            pltpu.VMEM((blocks * rows, columns), jnp.bfloat16),
            pltpu.VMEM((width, columns), jnp.bfloat16),
            pltpu.SemaphoreType.DMA((width // tile + 1,)),
        ],
        input_output_aliases=aliases,
        compiler_params=params(),
        cost_estimate=cost(1 << 20),
        name="grad",
    )(*operands)


def local(count, tokens, active_latent_index, latent_values, dec_bias, dec_weight):
    width, features = dec_weight.shape
    columns = features // 2
    first = (lax.axis_index("latent") * (width // LANES)).astype(jnp.int32).reshape(1)
    bias = dec_bias.reshape(1, features)

    def send(x):
        return lax.ppermute(x, "latent", ring_next(count))

    weight_a, own_table, a = begin(first, active_latent_index, latent_values, dec_weight, tokens, columns)
    weight_b, b = second(own_table, dec_weight, tokens, columns, columns)
    tables = [own_table]
    for k in range(1, count):
        last = k == count - 1
        table, a = step_a(first, send(a), weight_a, bias, last)
        b = step_b(table, send(b), weight_b, bias, columns, last)
        tables.append(table)
    errors = [[a], [b]]
    tables = [tables[-1]] + tables[:-1]
    split = max(1, count - 2)
    early = [None, None]
    for arrived in range(1, count):
        for c, chain in enumerate(errors):
            if arrived == count - 1:
                early[c] = early_grad(tables[:split], chain[:split])
                chain[-1], early[c] = lax.optimization_barrier((chain[-1], early[c]))
            chain.append(send(chain[-1]))
    made = None
    for chain, part, at in zip(errors, early, (0, columns)):
        made = grad_part(tables[split:], chain[split:], chain[1], part, features, at, made)
    return tuple(made)


def solution(mesh):
    in_specs = (
        P(("groups", "latent"), ("dp", "mp")),
        P(("groups", "latent"), None),
        P(("groups", "latent"), None),
        P(("groups", "dp", "mp")),
        P(("groups", "latent"), ("dp", "mp")),
    )
    out_specs = (P(("groups", "latent"), ("dp", "mp")), P(("groups", "latent"), ("dp", "mp")))
    body = functools.partial(local, mesh.shape["latent"])
    return jax.shard_map(body, mesh=mesh, in_specs=in_specs, out_specs=out_specs, check_vma=False)
```

```python
import functools

import jax
import jax.numpy as jnp
from jax import lax
from jax.experimental import pallas as pl
from jax.experimental.pallas import tpu as pltpu
from jax.sharding import PartitionSpec as P

LANES = 128
EXPONENT_BITS = (1, 2, 4, 8, 16, 32, 64)
GROUP = 8
TILE = 1024
LOAD_PARTS = 4
VMEM_LIMIT = 24 * 1024 * 1024
IN_VMEM = pl.BlockSpec(memory_space=pltpu.VMEM)
IN_SMEM = pl.BlockSpec(memory_space=pltpu.SMEM)
IN_HBM = pl.BlockSpec(memory_space=pltpu.HBM)


def params():
    return pltpu.CompilerParams(vmem_limit_bytes=VMEM_LIMIT)


def in_hbm(array):
    return pltpu.with_memory_space_constraint(array, pltpu.HBM)


def cost(byte_count):
    return pl.CostEstimate(flops=0, bytes_accessed=byte_count, transcendentals=0)


def ring_order(count):
    return [0] + list(range(2, count, 2)) + list(range(count - 1 - count % 2, 0, -2))


def ring_next(count):
    order = ring_order(count)
    return [(order[i], order[(i + 1) % count]) for i in range(count)]


def pack(ids, values, wide_ref):
    active, rows = ids.shape
    high = lax.shift_right_logical(ids, 7)
    low = jnp.bitwise_and(ids, LANES - 1)
    coded = 1.0 + low.astype(jnp.float32) * (1.0 / LANES)
    for bit in EXPONENT_BITS:
        coded = jnp.where(jnp.bitwise_and(high, bit) != 0, coded * 2.0**bit, coded)
    coded = jnp.where(high >= LANES, -coded, coded)
    wide_ref[0:rows, :] = coded.T
    wide_ref[rows:, :] = values.astype(jnp.float32).T
    even = wide_ref[pl.ds(0, rows, stride=2), :]
    odd = wide_ref[pl.ds(1, rows, stride=2), :]
    return jnp.concatenate([even, odd], axis=1)


def unpack_ids(coded):
    rest = jnp.abs(coded)
    high = jnp.where(coded < 0, LANES, 0)
    for bit in reversed(EXPONENT_BITS):
        over = rest >= 2.0**bit
        rest = jnp.where(over, rest * 2.0**-bit, rest)
        high = high + jnp.where(over, bit, 0)
    return high, ((rest - 1.0) * LANES).astype(jnp.int32)


def build_table(first, packed, table_ref, keys_ref):
    rows, width = table_ref.shape
    half = rows // 2
    per_row = 2
    rows_per_group = GROUP // per_row
    high_count = width // LANES
    high, low = unpack_ids(packed[0:half, :])
    high = high - first
    row = lax.broadcasted_iota(jnp.int32, high.shape, 0)
    lane = lax.broadcasted_iota(jnp.int32, high.shape, 1)
    place = per_row * jnp.bitwise_and(row, rows_per_group - 1) + jnp.where(lane >= LANES // 2, 1, 0)
    inside = jnp.logical_and(high >= 0, high < high_count)
    key = jnp.where(inside, high * GROUP + place, -1)
    keys_ref[0:half, :] = key.astype(jnp.float32)
    keys_ref[half : 2 * half, :] = low.astype(jnp.float32)
    keys_ref[2 * half :, :] = packed[half:, :]
    tall = lax.broadcasted_iota(jnp.int32, (high_count * GROUP, LANES), 0).astype(jnp.float32).astype(jnp.bfloat16)
    wide = lax.broadcasted_iota(jnp.int32, (LANES, LANES), 0).astype(jnp.float32).astype(jnp.bfloat16)
    zero, one = jnp.zeros((), jnp.bfloat16), jnp.ones((), jnp.bfloat16)

    def group_rows(r0):
        left, right = [], []
        for r in range(r0, r0 + rows_per_group):
            key = keys_ref[r : r + 1, :].astype(jnp.bfloat16)
            low = keys_ref[half + r : half + r + 1, :].astype(jnp.bfloat16)
            value = keys_ref[2 * half + r : 2 * half + r + 1, :].astype(jnp.bfloat16)
            left.append(jnp.where(tall == key, value, zero))
            right.append(jnp.where(wide == low, one, zero))
        left = jnp.concatenate(left, axis=1)
        right = jnp.concatenate(right, axis=1)
        product = lax.dot_general(left, right, (((1,), (1,)), ((), ())), preferred_element_type=jnp.float32)
        pieces = [product[h * GROUP : (h + 1) * GROUP, :] for h in range(high_count)]
        return jnp.concatenate(pieces, axis=1)

    for i in range(rows // (2 * GROUP)):
        r0 = i * (2 * rows_per_group)
        both = jnp.concatenate([group_rows(r0), group_rows(r0 + rows_per_group)], axis=0)
        table_ref[i * 2 * GROUP : (i + 1) * 2 * GROUP, :] = both.astype(jnp.bfloat16)


def multiply(table_ref, weight_ref, write):
    columns = weight_ref.shape[1]
    tile = min(TILE, columns)
    for c in range(0, columns, tile):
        at = slice(c, c + tile)
        write(at, jnp.dot(table_ref[...], weight_ref[:, at], preferred_element_type=jnp.float32))


def keys_scratch(rows):
    return pltpu.VMEM((rows + rows // 2, LANES), jnp.float32)


def start_loads(weight_hbm, tokens_hbm, column0, weight_ref, tokens_ref, sems):
    width, columns = weight_ref.shape
    part = width // LOAD_PARTS
    copies = []
    for i in range(LOAD_PARTS):
        rows = pl.ds(i * part, part)
        copies.append(
            pltpu.make_async_copy(weight_hbm.at[rows, pl.ds(column0, columns)], weight_ref.at[rows, :], sems.at[i])
        )
    copies.append(pltpu.make_async_copy(tokens_hbm.at[:, pl.ds(column0, columns)], tokens_ref, sems.at[LOAD_PARTS]))
    for copy in copies:
        copy.start()
    return copies


def multiply_loaded(copies, table_ref, weight_ref, tokens_ref):
    part = weight_ref.shape[0] // LOAD_PARTS
    total = None
    for i in range(LOAD_PARTS):
        copies[i].wait()
        at = slice(i * part, (i + 1) * part)
        product = jnp.dot(table_ref[:, at], weight_ref[at, :], preferred_element_type=jnp.float32)
        total = product if total is None else total + product
    copies[LOAD_PARTS].wait()
    return total - tokens_ref[...].astype(jnp.float32)


def begin_kernel(
    first_ref, ids_hbm, values_hbm, weight_hbm, tokens_hbm,
    weight_ref, table_ref, message_ref,
    ids_ref, values_ref, wide_ref, keys_ref, tokens_ref, sems,
):
    small = [
        pltpu.make_async_copy(ids_hbm, ids_ref, sems.at[LOAD_PARTS + 1]),
        pltpu.make_async_copy(values_hbm, values_ref, sems.at[LOAD_PARTS + 2]),
    ]
    for copy in small:
        copy.start()
    copies = start_loads(weight_hbm, tokens_hbm, 0, weight_ref, tokens_ref, sems)
    for copy in small:
        copy.wait()
    packed = pack(ids_ref[...], values_ref[...], wide_ref)
    columns = weight_ref.shape[1]
    message_ref[:, columns:] = packed.astype(message_ref.dtype)
    build_table(first_ref[0], packed, table_ref, keys_ref)
    total = multiply_loaded(copies, table_ref, weight_ref, tokens_ref)
    message_ref[:, :columns] = total.astype(message_ref.dtype)


def begin(first, ids, values, weight, tokens, columns):
    width = weight.shape[0]
    rows, active = ids.shape
    return pl.pallas_call(
        begin_kernel,
        in_specs=[IN_SMEM] + [IN_HBM] * 4,
        out_specs=[IN_VMEM] * 3,
        out_shape=[
            jax.ShapeDtypeStruct((width, columns), weight.dtype),
            jax.ShapeDtypeStruct((rows, width), jnp.bfloat16),
            jax.ShapeDtypeStruct((rows, columns + 2 * active), jnp.bfloat16),
        ],
        scratch_shapes=[
            pltpu.VMEM((active, rows), ids.dtype),
            pltpu.VMEM((active, rows), values.dtype),
            pltpu.VMEM((2 * rows, active), jnp.float32),
            keys_scratch(rows),
            pltpu.VMEM((rows, columns), tokens.dtype),
            pltpu.SemaphoreType.DMA((LOAD_PARTS + 3,)),
        ],
        compiler_params=params(),
        cost_estimate=cost(1 << 20),
        name="begin",
    )(first, in_hbm(ids.T), in_hbm(values.T), in_hbm(weight), in_hbm(tokens))


def second_kernel(column0, table_ref, weight_hbm, tokens_hbm, weight_ref, out_ref, tokens_ref, sems):
    copies = start_loads(weight_hbm, tokens_hbm, column0, weight_ref, tokens_ref, sems)
    out_ref[...] = multiply_loaded(copies, table_ref, weight_ref, tokens_ref).astype(out_ref.dtype)


def second(table, weight, tokens, column0, columns):
    width = weight.shape[0]
    rows = tokens.shape[0]
    return pl.pallas_call(
        functools.partial(second_kernel, column0),
        in_specs=[IN_VMEM, IN_HBM, IN_HBM],
        out_specs=[IN_VMEM] * 2,
        out_shape=[
            jax.ShapeDtypeStruct((width, columns), weight.dtype),
            jax.ShapeDtypeStruct((rows, columns), jnp.bfloat16),
        ],
        scratch_shapes=[
            pltpu.VMEM((rows, columns), tokens.dtype),
            pltpu.SemaphoreType.DMA((LOAD_PARTS + 1,)),
        ],
        compiler_params=params(),
        cost_estimate=cost(1 << 20),
        name="second",
    )(table, in_hbm(weight), in_hbm(tokens))


def step_kernel(last, first_ref, arrived_ref, weight_ref, bias_ref, table_ref, out_ref, keys_ref):
    columns = weight_ref.shape[1]
    build_table(first_ref[0], arrived_ref[:, columns:].astype(jnp.float32), table_ref, keys_ref)
    if not last:
        out_ref[:, columns:] = arrived_ref[:, columns:]

    def write(at, product):
        total = product + arrived_ref[:, at].astype(jnp.float32)
        if last:
            total = total + bias_ref[:, at]
        out_ref[:, at] = total.astype(out_ref.dtype)

    multiply(table_ref, weight_ref, write)


def step_a(first, arrived, weight, bias, last):
    width, columns = weight.shape
    rows = arrived.shape[0]
    return pl.pallas_call(
        functools.partial(step_kernel, last),
        in_specs=[IN_SMEM] + [IN_VMEM] * 3,
        out_specs=[IN_VMEM] * 2,
        out_shape=[
            jax.ShapeDtypeStruct((rows, width), jnp.bfloat16),
            jax.ShapeDtypeStruct((rows, columns if last else arrived.shape[1]), jnp.bfloat16),
        ],
        scratch_shapes=[keys_scratch(rows)],
        compiler_params=params(),
        cost_estimate=cost(1 << 20),
        name="step_a",
    )(first, arrived, weight, bias)


def multiply_kernel(table_ref, weight_ref, out_ref):
    def write(at, product):
        out_ref[:, at] = product

    multiply(table_ref, weight_ref, write)


def add_kernel(column0, last, part_ref, arrived_ref, bias_ref, out_ref):
    total = part_ref[...] + arrived_ref[...].astype(jnp.float32)
    if last:
        total = total + bias_ref[:, column0 : column0 + part_ref.shape[1]]
    out_ref[...] = total.astype(out_ref.dtype)


def step_b(table, arrived, weight, bias, column0, last):
    shape = arrived.shape
    part = pl.pallas_call(
        multiply_kernel,
        in_specs=[IN_VMEM] * 2,
        out_specs=IN_VMEM,
        out_shape=jax.ShapeDtypeStruct(shape, jnp.float32),
        compiler_params=params(),
        cost_estimate=cost(1 << 20),
        name="multiply",
    )(table, weight)
    return pl.pallas_call(
        functools.partial(add_kernel, column0, last),
        in_specs=[IN_VMEM] * 3,
        out_specs=IN_VMEM,
        out_shape=jax.ShapeDtypeStruct(shape, jnp.bfloat16),
        compiler_params=params(),
        cost_estimate=cost(1 << 20),
        name="add",
    )(part, arrived, bias)


def contract_tokens(tables, all_ref, at):
    table = jnp.concatenate([table_ref[:, at] for table_ref in tables], axis=0)
    return lax.dot_general(table, all_ref[...], (((0,), (0,)), ((), ())), preferred_element_type=jnp.float32)


def gather_errors(errors, all_ref):
    rows = errors[0].shape[0]
    for b, error_ref in enumerate(errors):
        all_ref[b * rows : (b + 1) * rows, :] = error_ref[...]


def early_kernel(blocks, tile, *refs):
    tables, errors, out_ref, all_ref = refs[:blocks], refs[blocks : 2 * blocks], refs[-2], refs[-1]
    gather_errors(errors, all_ref)
    for l in range(0, out_ref.shape[0], tile):
        at = slice(l, l + tile)
        out_ref[at, :] = contract_tokens(tables, all_ref, at)


def early_grad(tables, errors, tile=512):
    width = tables[0].shape[1]
    rows, columns = errors[0].shape
    blocks = len(errors)
    return pl.pallas_call(
        functools.partial(early_kernel, blocks, tile),
        in_specs=[IN_VMEM] * (2 * blocks),
        out_specs=IN_VMEM,
        out_shape=jax.ShapeDtypeStruct((width, columns), jnp.float32),
        scratch_shapes=[pltpu.VMEM((blocks * rows, columns), jnp.bfloat16)],
        compiler_params=params(),
        cost_estimate=cost(1 << 20),
        name="early_grad",
    )(*tables, *errors)


def grad_kernel(blocks, column0, tile, *refs):
    tables, errors, (own_ref, early_ref) = refs[:blocks], refs[blocks : 2 * blocks], refs[2 * blocks : 2 * blocks + 2]
    error_out, grad_out, all_ref, made_ref, sems = refs[-5:]
    rows, columns = errors[0].shape
    width = tables[0].shape[1]
    part = pl.ds(column0, columns)
    copies = [pltpu.make_async_copy(own_ref, error_out.at[:, part], sems.at[width // tile])]
    copies[0].start()
    gather_errors(errors, all_ref)
    for i, l in enumerate(range(0, width, tile)):
        at = slice(l, l + tile)
        product = contract_tokens(tables, all_ref, at) + early_ref[at, :]
        made_ref[at, :] = product.astype(made_ref.dtype)
        copy = pltpu.make_async_copy(made_ref.at[pl.ds(l, tile), :], grad_out.at[pl.ds(l, tile), part], sems.at[i])
        copy.start()
        copies.append(copy)
    for copy in copies:
        copy.wait()


def grad_part(tables, errors, own, early, features, column0, previous, tile=128):
    width = tables[0].shape[1]
    rows, columns = errors[0].shape
    blocks = len(errors)
    in_specs = [IN_VMEM] * (2 * blocks + 2)
    operands = [*tables, *errors, own, early]
    aliases = {}
    if previous is not None:
        aliases = {len(operands): 0, len(operands) + 1: 1}
        in_specs += [IN_HBM, IN_HBM]
        operands += previous
    return pl.pallas_call(
        functools.partial(grad_kernel, blocks, column0, tile),
        in_specs=in_specs,
        out_specs=[IN_HBM, IN_HBM],
        out_shape=[
            jax.ShapeDtypeStruct((rows, features), jnp.bfloat16),
            jax.ShapeDtypeStruct((width, features), jnp.bfloat16),
        ],
        scratch_shapes=[
            pltpu.VMEM((blocks * rows, columns), jnp.bfloat16),
            pltpu.VMEM((width, columns), jnp.bfloat16),
            pltpu.SemaphoreType.DMA((width // tile + 1,)),
        ],
        input_output_aliases=aliases,
        compiler_params=params(),
        cost_estimate=cost(1 << 20),
        name="grad",
    )(*operands)


def local(count, tokens, active_latent_index, latent_values, dec_bias, dec_weight):
    width, features = dec_weight.shape
    columns = features // 2
    first = (lax.axis_index("latent") * (width // LANES)).astype(jnp.int32).reshape(1)
    bias = dec_bias.reshape(1, features)

    def send(x):
        return lax.ppermute(x, "latent", ring_next(count))

    weight_a, own_table, a = begin(first, active_latent_index, latent_values, dec_weight, tokens, columns)
    weight_b, b = second(own_table, dec_weight, tokens, columns, columns)
    tables = [own_table]
    for k in range(1, count):
        last = k == count - 1
        table, a = step_a(first, send(a), weight_a, bias, last)
        b = step_b(table, send(b), weight_b, bias, columns, last)
        tables.append(table)
    errors = [[a], [b]]
    tables = [tables[-1]] + tables[:-1]
    split = max(1, count - 2)
    early = [None, None]
    for arrived in range(1, count):
        for c, chain in enumerate(errors):
            if arrived == count - 1:
                early[c] = early_grad(tables[:split], chain[:split])
                chain[-1], early[c] = lax.optimization_barrier((chain[-1], early[c]))
            chain.append(send(chain[-1]))
    made = None
    for chain, part, at in zip(errors, early, (0, columns)):
        made = grad_part(tables[split:], chain[split:], chain[1], part, features, at, made)
    return tuple(made)


def solution(mesh):
    in_specs = (
        P(("groups", "latent"), ("dp", "mp")),
        P(("groups", "latent"), None),
        P(("groups", "latent"), None),
        P(("groups", "dp", "mp")),
        P(("groups", "latent"), ("dp", "mp")),
    )
    out_specs = (P(("groups", "latent"), ("dp", "mp")), P(("groups", "latent"), ("dp", "mp")))
    body = functools.partial(local, mesh.shape["latent"])
    return jax.shard_map(body, mesh=mesh, in_specs=in_specs, out_specs=out_specs, check_vma=False)
```

```python
import functools

import jax
import jax.numpy as jnp
from jax import lax
from jax.experimental import pallas as pl
from jax.experimental.pallas import tpu as pltpu
from jax.sharding import PartitionSpec as P

LANES = 128
EXPONENT_BITS = (1, 2, 4, 8, 16, 32, 64)
GROUP = 8
TILE = 1024
LOAD_PARTS = 4
VMEM_LIMIT = 24 * 1024 * 1024
IN_VMEM = pl.BlockSpec(memory_space=pltpu.VMEM)
IN_SMEM = pl.BlockSpec(memory_space=pltpu.SMEM)
IN_HBM = pl.BlockSpec(memory_space=pltpu.HBM)


def params():
    return pltpu.CompilerParams(vmem_limit_bytes=VMEM_LIMIT)


def in_hbm(array):
    return pltpu.with_memory_space_constraint(array, pltpu.HBM)


def cost(byte_count):
    return pl.CostEstimate(flops=0, bytes_accessed=byte_count, transcendentals=0)


def ring_order(count):
    return [0] + list(range(2, count, 2)) + list(range(count - 1 - count % 2, 0, -2))


def ring_next(count):
    order = ring_order(count)
    return [(order[i], order[(i + 1) % count]) for i in range(count)]


def pack(ids, values, wide_ref):
    active, rows = ids.shape
    high = lax.shift_right_logical(ids, 7)
    low = jnp.bitwise_and(ids, LANES - 1)
    coded = 1.0 + low.astype(jnp.float32) * (1.0 / LANES)
    for bit in EXPONENT_BITS:
        coded = jnp.where(jnp.bitwise_and(high, bit) != 0, coded * 2.0**bit, coded)
    coded = jnp.where(high >= LANES, -coded, coded)
    wide_ref[0:rows, :] = coded.T
    wide_ref[rows:, :] = values.astype(jnp.float32).T
    even = wide_ref[pl.ds(0, rows, stride=2), :]
    odd = wide_ref[pl.ds(1, rows, stride=2), :]
    return jnp.concatenate([even, odd], axis=1)


def unpack_ids(coded):
    rest = jnp.abs(coded)
    high = jnp.where(coded < 0, LANES, 0)
    for bit in reversed(EXPONENT_BITS):
        over = rest >= 2.0**bit
        rest = jnp.where(over, rest * 2.0**-bit, rest)
        high = high + jnp.where(over, bit, 0)
    return high, ((rest - 1.0) * LANES).astype(jnp.int32)


def build_table(first, packed, table_ref, keys_ref):
    rows, width = table_ref.shape
    half = rows // 2
    per_row = 2
    rows_per_group = GROUP // per_row
    high_count = width // LANES
    high, low = unpack_ids(packed[0:half, :])
    high = high - first
    row = lax.broadcasted_iota(jnp.int32, high.shape, 0)
    lane = lax.broadcasted_iota(jnp.int32, high.shape, 1)
    place = per_row * jnp.bitwise_and(row, rows_per_group - 1) + jnp.where(lane >= LANES // 2, 1, 0)
    inside = jnp.logical_and(high >= 0, high < high_count)
    key = jnp.where(inside, high * GROUP + place, -1)
    keys_ref[0:half, :] = key.astype(jnp.float32)
    keys_ref[half : 2 * half, :] = low.astype(jnp.float32)
    keys_ref[2 * half :, :] = packed[half:, :]
    tall = lax.broadcasted_iota(jnp.int32, (high_count * GROUP, LANES), 0).astype(jnp.float32).astype(jnp.bfloat16)
    wide = lax.broadcasted_iota(jnp.int32, (LANES, LANES), 0).astype(jnp.float32).astype(jnp.bfloat16)
    zero, one = jnp.zeros((), jnp.bfloat16), jnp.ones((), jnp.bfloat16)

    def group_rows(r0):
        left, right = [], []
        for r in range(r0, r0 + rows_per_group):
            key = keys_ref[r : r + 1, :].astype(jnp.bfloat16)
            low = keys_ref[half + r : half + r + 1, :].astype(jnp.bfloat16)
            value = keys_ref[2 * half + r : 2 * half + r + 1, :].astype(jnp.bfloat16)
            left.append(jnp.where(tall == key, value, zero))
            right.append(jnp.where(wide == low, one, zero))
        left = jnp.concatenate(left, axis=1)
        right = jnp.concatenate(right, axis=1)
        product = lax.dot_general(left, right, (((1,), (1,)), ((), ())), preferred_element_type=jnp.float32)
        pieces = [product[h * GROUP : (h + 1) * GROUP, :] for h in range(high_count)]
        return jnp.concatenate(pieces, axis=1)

    for i in range(rows // (2 * GROUP)):
        r0 = i * (2 * rows_per_group)
        both = jnp.concatenate([group_rows(r0), group_rows(r0 + rows_per_group)], axis=0)
        table_ref[i * 2 * GROUP : (i + 1) * 2 * GROUP, :] = both.astype(jnp.bfloat16)


def multiply(table_ref, weight_ref, write):
    columns = weight_ref.shape[1]
    tile = min(TILE, columns)
    for c in range(0, columns, tile):
        at = slice(c, c + tile)
        write(at, jnp.dot(table_ref[...], weight_ref[:, at], preferred_element_type=jnp.float32))


def keys_scratch(rows):
    return pltpu.VMEM((rows + rows // 2, LANES), jnp.float32)


def start_loads(weight_hbm, tokens_hbm, column0, weight_ref, tokens_ref, sems):
    width, columns = weight_ref.shape
    part = width // LOAD_PARTS
    copies = []
    for i in range(LOAD_PARTS):
        rows = pl.ds(i * part, part)
        copies.append(
            pltpu.make_async_copy(weight_hbm.at[rows, pl.ds(column0, columns)], weight_ref.at[rows, :], sems.at[i])
        )
    copies.append(pltpu.make_async_copy(tokens_hbm.at[:, pl.ds(column0, columns)], tokens_ref, sems.at[LOAD_PARTS]))
    for copy in copies:
        copy.start()
    return copies


def multiply_loaded(copies, table_ref, weight_ref, tokens_ref):
    part = weight_ref.shape[0] // LOAD_PARTS
    total = None
    for i in range(LOAD_PARTS):
        copies[i].wait()
        at = slice(i * part, (i + 1) * part)
        product = jnp.dot(table_ref[:, at], weight_ref[at, :], preferred_element_type=jnp.float32)
        total = product if total is None else total + product
    copies[LOAD_PARTS].wait()
    return total - tokens_ref[...].astype(jnp.float32)


def begin_kernel(
    first_ref, ids_hbm, values_hbm, weight_hbm, tokens_hbm,
    weight_ref, table_ref, message_ref,
    ids_ref, values_ref, wide_ref, keys_ref, tokens_ref, sems,
):
    small = [
        pltpu.make_async_copy(ids_hbm, ids_ref, sems.at[LOAD_PARTS + 1]),
        pltpu.make_async_copy(values_hbm, values_ref, sems.at[LOAD_PARTS + 2]),
    ]
    for copy in small:
        copy.start()
    copies = start_loads(weight_hbm, tokens_hbm, 0, weight_ref, tokens_ref, sems)
    for copy in small:
        copy.wait()
    packed = pack(ids_ref[...], values_ref[...], wide_ref)
    columns = weight_ref.shape[1]
    message_ref[:, columns:] = packed.astype(message_ref.dtype)
    build_table(first_ref[0], packed, table_ref, keys_ref)
    total = multiply_loaded(copies, table_ref, weight_ref, tokens_ref)
    message_ref[:, :columns] = total.astype(message_ref.dtype)


def begin(first, ids, values, weight, tokens, columns):
    width = weight.shape[0]
    rows, active = ids.shape
    return pl.pallas_call(
        begin_kernel,
        in_specs=[IN_SMEM] + [IN_HBM] * 4,
        out_specs=[IN_VMEM] * 3,
        out_shape=[
            jax.ShapeDtypeStruct((width, columns), weight.dtype),
            jax.ShapeDtypeStruct((rows, width), jnp.bfloat16),
            jax.ShapeDtypeStruct((rows, columns + 2 * active), jnp.bfloat16),
        ],
        scratch_shapes=[
            pltpu.VMEM((active, rows), ids.dtype),
            pltpu.VMEM((active, rows), values.dtype),
            pltpu.VMEM((2 * rows, active), jnp.float32),
            keys_scratch(rows),
            pltpu.VMEM((rows, columns), tokens.dtype),
            pltpu.SemaphoreType.DMA((LOAD_PARTS + 3,)),
        ],
        compiler_params=params(),
        cost_estimate=cost(1 << 20),
        name="begin",
    )(first, in_hbm(ids.T), in_hbm(values.T), in_hbm(weight), in_hbm(tokens))


def second_kernel(column0, table_ref, weight_hbm, tokens_hbm, weight_ref, out_ref, tokens_ref, sems):
    copies = start_loads(weight_hbm, tokens_hbm, column0, weight_ref, tokens_ref, sems)
    out_ref[...] = multiply_loaded(copies, table_ref, weight_ref, tokens_ref).astype(out_ref.dtype)


def second(table, weight, tokens, column0, columns):
    width = weight.shape[0]
    rows = tokens.shape[0]
    return pl.pallas_call(
        functools.partial(second_kernel, column0),
        in_specs=[IN_VMEM, IN_HBM, IN_HBM],
        out_specs=[IN_VMEM] * 2,
        out_shape=[
            jax.ShapeDtypeStruct((width, columns), weight.dtype),
            jax.ShapeDtypeStruct((rows, columns), jnp.bfloat16),
        ],
        scratch_shapes=[
            pltpu.VMEM((rows, columns), tokens.dtype),
            pltpu.SemaphoreType.DMA((LOAD_PARTS + 1,)),
        ],
        compiler_params=params(),
        cost_estimate=cost(1 << 20),
        name="second",
    )(table, in_hbm(weight), in_hbm(tokens))


def step_kernel(last, first_ref, arrived_ref, weight_ref, bias_ref, table_ref, out_ref, keys_ref):
    columns = weight_ref.shape[1]
    build_table(first_ref[0], arrived_ref[:, columns:].astype(jnp.float32), table_ref, keys_ref)
    if not last:
        out_ref[:, columns:] = arrived_ref[:, columns:]

    def write(at, product):
        total = product + arrived_ref[:, at].astype(jnp.float32)
        if last:
            total = total + bias_ref[:, at]
        out_ref[:, at] = total.astype(out_ref.dtype)

    multiply(table_ref, weight_ref, write)


def step_a(first, arrived, weight, bias, last):
    width, columns = weight.shape
    rows = arrived.shape[0]
    return pl.pallas_call(
        functools.partial(step_kernel, last),
        in_specs=[IN_SMEM] + [IN_VMEM] * 3,
        out_specs=[IN_VMEM] * 2,
        out_shape=[
            jax.ShapeDtypeStruct((rows, width), jnp.bfloat16),
            jax.ShapeDtypeStruct((rows, columns if last else arrived.shape[1]), jnp.bfloat16),
        ],
        scratch_shapes=[keys_scratch(rows)],
        compiler_params=params(),
        cost_estimate=cost(1 << 20),
        name="step_a",
    )(first, arrived, weight, bias)


def multiply_kernel(table_ref, weight_ref, out_ref):
    def write(at, product):
        out_ref[:, at] = product

    multiply(table_ref, weight_ref, write)


def add_kernel(column0, last, part_ref, arrived_ref, bias_ref, out_ref):
    total = part_ref[...] + arrived_ref[...].astype(jnp.float32)
    if last:
        total = total + bias_ref[:, column0 : column0 + part_ref.shape[1]]
    out_ref[...] = total.astype(out_ref.dtype)


def step_b(table, arrived, weight, bias, column0, last):
    shape = arrived.shape
    part = pl.pallas_call(
        multiply_kernel,
        in_specs=[IN_VMEM] * 2,
        out_specs=IN_VMEM,
        out_shape=jax.ShapeDtypeStruct(shape, jnp.float32),
        compiler_params=params(),
        cost_estimate=cost(1 << 20),
        name="multiply",
    )(table, weight)
    return pl.pallas_call(
        functools.partial(add_kernel, column0, last),
        in_specs=[IN_VMEM] * 3,
        out_specs=IN_VMEM,
        out_shape=jax.ShapeDtypeStruct(shape, jnp.bfloat16),
        compiler_params=params(),
        cost_estimate=cost(1 << 20),
        name="add",
    )(part, arrived, bias)


def contract_tokens(tables, errors, at):
    table = jnp.concatenate([table_ref[:, at] for table_ref in tables], axis=0)
    stacked = jnp.concatenate([error_ref[...] for error_ref in errors], axis=0)
    return lax.dot_general(table, stacked, (((0,), (0,)), ((), ())), preferred_element_type=jnp.float32)


def early_kernel(blocks, tile, *refs):
    tables, errors, out_ref = refs[:blocks], refs[blocks : 2 * blocks], refs[-1]
    for l in range(0, out_ref.shape[0], tile):
        at = slice(l, l + tile)
        out_ref[at, :] = contract_tokens(tables, errors, at)


def early_grad(tables, errors, tile=512):
    width = tables[0].shape[1]
    rows, columns = errors[0].shape
    blocks = len(errors)
    return pl.pallas_call(
        functools.partial(early_kernel, blocks, tile),
        in_specs=[IN_VMEM] * (2 * blocks),
        out_specs=IN_VMEM,
        out_shape=jax.ShapeDtypeStruct((width, columns), jnp.float32),
        compiler_params=params(),
        cost_estimate=cost(1 << 20),
        name="early_grad",
    )(*tables, *errors)


def grad_kernel(blocks, column0, tile, *refs):
    tables, errors, (own_ref, early_ref) = refs[:blocks], refs[blocks : 2 * blocks], refs[2 * blocks : 2 * blocks + 2]
    error_out, grad_out, made_ref, sems = refs[-4:]
    rows, columns = errors[0].shape
    width = tables[0].shape[1]
    part = pl.ds(column0, columns)
    copies = [pltpu.make_async_copy(own_ref, error_out.at[:, part], sems.at[width // tile])]
    copies[0].start()
    for i, l in enumerate(range(0, width, tile)):
        at = slice(l, l + tile)
        product = contract_tokens(tables, errors, at) + early_ref[at, :]
        made_ref[at, :] = product.astype(made_ref.dtype)
        copy = pltpu.make_async_copy(made_ref.at[pl.ds(l, tile), :], grad_out.at[pl.ds(l, tile), part], sems.at[i])
        copy.start()
        copies.append(copy)
    for copy in copies:
        copy.wait()


def grad_part(tables, errors, own, early, features, column0, previous, tile=128):
    width = tables[0].shape[1]
    rows, columns = errors[0].shape
    blocks = len(errors)
    in_specs = [IN_VMEM] * (2 * blocks + 2)
    operands = [*tables, *errors, own, early]
    aliases = {}
    if previous is not None:
        aliases = {len(operands): 0, len(operands) + 1: 1}
        in_specs += [IN_HBM, IN_HBM]
        operands += previous
    return pl.pallas_call(
        functools.partial(grad_kernel, blocks, column0, tile),
        in_specs=in_specs,
        out_specs=[IN_HBM, IN_HBM],
        out_shape=[
            jax.ShapeDtypeStruct((rows, features), jnp.bfloat16),
            jax.ShapeDtypeStruct((width, features), jnp.bfloat16),
        ],
        scratch_shapes=[
            pltpu.VMEM((width, columns), jnp.bfloat16),
            pltpu.SemaphoreType.DMA((width // tile + 1,)),
        ],
        input_output_aliases=aliases,
        compiler_params=params(),
        cost_estimate=cost(1 << 20),
        name="grad",
    )(*operands)


def local(count, tokens, active_latent_index, latent_values, dec_bias, dec_weight):
    width, features = dec_weight.shape
    columns = features // 2
    first = (lax.axis_index("latent") * (width // LANES)).astype(jnp.int32).reshape(1)
    bias = dec_bias.reshape(1, features)

    def send(x):
        return lax.ppermute(x, "latent", ring_next(count))

    weight_a, own_table, a = begin(first, active_latent_index, latent_values, dec_weight, tokens, columns)
    weight_b, b = second(own_table, dec_weight, tokens, columns, columns)
    tables = [own_table]
    for k in range(1, count):
        last = k == count - 1
        table, a = step_a(first, send(a), weight_a, bias, last)
        b = step_b(table, send(b), weight_b, bias, columns, last)
        tables.append(table)
    errors = [[a], [b]]
    tables = [tables[-1]] + tables[:-1]
    split = max(1, count - 2)
    early = [None, None]
    for arrived in range(1, count):
        for c, chain in enumerate(errors):
            if arrived == count - 1:
                early[c] = early_grad(tables[:split], chain[:split])
                chain[-1], early[c] = lax.optimization_barrier((chain[-1], early[c]))
            chain.append(send(chain[-1]))
    made = None
    for chain, part, at in zip(errors, early, (0, columns)):
        made = grad_part(tables[split:], chain[split:], chain[1], part, features, at, made)
    return tuple(made)


def solution(mesh):
    in_specs = (
        P(("groups", "latent"), ("dp", "mp")),
        P(("groups", "latent"), None),
        P(("groups", "latent"), None),
        P(("groups", "dp", "mp")),
        P(("groups", "latent"), ("dp", "mp")),
    )
    out_specs = (P(("groups", "latent"), ("dp", "mp")), P(("groups", "latent"), ("dp", "mp")))
    body = functools.partial(local, mesh.shape["latent"])
    return jax.shard_map(body, mesh=mesh, in_specs=in_specs, out_specs=out_specs, check_vma=False)
```
